128 devices in a mesh: member: 16 (over y, x_lo, core), tp: 8 (over x_hi, z).
Axes of the slice: x: 4 (x_hi: 2, x_lo: 2; x = x_hi * 2 + x_lo), y: 4, z: 4, core: 2. Of those that a mesh axis runs over, the one named last changes fastest.
Arguments:
- acts: bfloat16 [16, 512, 2560], P('member', None, 'tp'), may hold values from -8 to 8
- weights: bfloat16 [16, 2560, 1024], P('member', 'tp'), may hold values from -6 to 6
Outputs:
- merged: bfloat16 [2560, 1024], P(None, 'tp')
The draws below stay inside these ranges and needn't reach their ends.
All inputs are finite; a program needn't handle non-finite values.
Results may differ from the reference program's by a relative error of at most 0.005.
Values may be sent and summed in bfloat16 or wider, within the bound.
A program may use at most 256 MiB of HBM per device.

```python
import math
import jax
import jax.numpy as jnp
from jax import lax

D = 2560
ROWS = 512
MEMBERS = 16
COLS = 1024


def draw_acts(key, part):
    key = jax.random.fold_in(key, 11)
    levels = 0
    while levels < 9 and D % 2 ** (levels + 1) == 0 and (D // 2 ** (levels + 1) >= 2):
        levels = levels + 1
    spread = 1.0
    mean_power = math.sinh(2.0) / 2.0
    summed = jnp.zeros((MEMBERS, ROWS, D), jnp.float32)
    for level in range(levels + 1):
        groups = 2 ** level
        level_key = jax.random.fold_in(key, 100 + level)
        scale_key, value_key = jax.random.split(level_key)
        amplitude = jnp.exp(jax.random.uniform(scale_key, (groups,), jnp.float32, -spread, spread))
        latent = jax.random.normal(value_key, (MEMBERS, ROWS, groups), jnp.float32)
        summed = summed + jnp.repeat(latent * amplitude, D // groups, axis=2)
    noise_key, sign_key, width_key, order_key = jax.random.split(key, 4)
    noise = jax.random.normal(noise_key, (MEMBERS, ROWS, D), jnp.float32)
    summed = (summed + noise) / math.sqrt((levels + 1) * mean_power + 1.0)
    signs = 2.0 * jax.random.randint(sign_key, (D,), 0, 2).astype(jnp.float32) - 1.0
    feature_scale = signs * jnp.exp(jax.random.uniform(width_key, (D,), jnp.float32, -0.4, 0.4))
    summed = summed * feature_scale
    order = jax.random.permutation(order_key, D)
    summed = jnp.take(summed, order, axis=2)
    return jnp.clip(summed, -8.0, 8.0).astype(jnp.bfloat16)


def block_levels(own_key, dims, cuts, least, high):
    gain, own = 1.0, jax.random.fold_in(own_key, 6)
    for position, shards_of in cuts:
        draws = jnp.exp(jax.random.uniform(jax.random.fold_in(own, position), (shards_of,), jnp.float32, least / len(cuts), high / len(cuts)))
        gain = gain * jnp.repeat(draws, dims[position] // shards_of).reshape([-1 if axis == position else 1 for axis in range(len(dims))])
    return gain


def centred(own_key, dims, width, reach, cuts=(), kind=jnp.bfloat16):
    loudness = block_levels(own_key, dims, cuts, -0.22, 0.18) if cuts else 1.0
    result = jax.random.normal(own_key, dims, jnp.float32) * width * loudness
    return jnp.minimum(jnp.maximum(result, -reach), reach).astype(kind)


def setup_inputs(seed: int = 0) -> dict:
    key_of = jax.random.split(jax.random.key(seed), 3)
    acts = draw_acts(jax.random.fold_in(key_of[2], 71), 0)
    weights = centred(key_of[1], (MEMBERS, D, COLS), 1.0, 6.0, ((0, 16), (1, 8)))
    return dict(acts=acts, weights=weights)


shrink = 0.9

def reference(acts, weights):

    def accumulate(totals, member_pair):
        gram_sum, right_sum = totals
        member_acts, weight = member_pair
        member_gram = jnp.dot(member_acts.T.astype(jnp.float32), member_acts.astype(jnp.float32), preferred_element_type=jnp.float32)
        gram_diag = jnp.diagonal(member_gram)
        projected = jnp.dot(member_acts.astype(jnp.float32), weight.astype(jnp.float32), preferred_element_type=jnp.float32).astype(jnp.bfloat16)
        member_right = shrink * jnp.dot(member_acts.T.astype(jnp.float32), projected.astype(jnp.float32), preferred_element_type=jnp.float32)
        member_right = member_right + (1.0 - shrink) * gram_diag[:, None] * weight.astype(jnp.float32)
        return ((gram_sum + member_gram, right_sum + member_right), None)
    start_totals = (jnp.zeros((D, D), jnp.float32), jnp.zeros((D, COLS), jnp.float32))
    (gram_total, right_total), _ = lax.scan(accumulate, start_totals, (acts, weights))
    on_diagonal = jnp.eye(D, dtype=bool)
    merged_gram = jnp.where(on_diagonal, gram_total, shrink * gram_total)
    factor = jnp.linalg.cholesky(merged_gram)
    solution = jax.scipy.linalg.cho_solve((factor, True), right_total)
    return solution.astype(jnp.bfloat16)
```

```python
import jax
import jax.numpy as jnp
from jax import lax
from jax.experimental import pallas as pl
from jax.experimental.pallas import tpu as pltpu
from jax.sharding import PartitionSpec as P

f32, bf16 = jnp.float32, jnp.bfloat16
SHRINK = 0.9
B = 256
H = 128
NT = (((1,), (1,)), ((), ()))
NN = (((1,), (0,)), ((), ()))
TN = (((0,), (0,)), ((), ()))


def split(x):
    hi = x.astype(bf16)
    return hi, (x - hi.astype(f32)).astype(bf16)


def mm(a, b, dims=NN):
    return lax.dot_general(a, b, dims, preferred_element_type=f32)


def mm3(a, b, dims=NN):
    ah, al = split(a)
    bh, bl = split(b)
    return mm(ah, bh, dims) + (mm(ah, bl, dims) + mm(al, bh, dims))


def recip(d):
    r = pl.reciprocal(d, approx=True)
    r = r * (2.0 - d * r)
    return r * (2.0 - d * r)


def inverse_factor(block):
    groups = H // 8
    lane = lax.broadcasted_iota(jnp.int32, (8, H), 1)
    sub = lax.broadcasted_iota(jnp.int32, (8, H), 0)
    a = [block[8 * g : 8 * g + 8, :] for g in range(groups)]
    out = []
    for t in range(groups):
        base = 8 * t
        slab = a[t]
        in_block = (lane >= base) & (lane < base + 8)
        rows = [jnp.broadcast_to(slab[i : i + 1, :], (8, H)) for i in range(8)]
        e = [
            [jnp.broadcast_to(rows[i][:, base + c : base + c + 1], (8, H)) for c in range(i + 1)]
            for i in range(8)
        ]
        r = [jnp.where(in_block, (lane == base + i).astype(f32), rows[i]) for i in range(8)]
        inv = [None] * 8
        low = [[None] * 8 for _ in range(8)]
        for c in range(8):
            inv[c] = recip(e[c][c])
            for i in range(c + 1, 8):
                low[i][c] = e[i][c] * inv[c]
            for i in range(c + 1, 8):
                for j in range(c + 1, i + 1):
                    e[i][j] = e[i][j] - low[i][c] * e[j][c]
                r[i] = r[i] - low[i][c] * r[c]
        own = jnp.zeros((8, H), f32)
        for i in range(8):
            own = jnp.where(sub == i, r[i] * lax.rsqrt(e[i][i]), own)
        out.append(jnp.where(lane < base + 8, own, 0.0))
        if t + 1 < groups:
            z = [r[i] * inv[i] for i in range(8)]
            for i in range(7, 0, -1):
                for j in range(i):
                    z[j] = z[j] - low[i][j] * z[i]
            for g in range(t + 1, groups):
                new = jnp.where(in_block, 0.0, a[g])
                for j in range(8):
                    new = new - jnp.broadcast_to(a[g][:, base + j : base + j + 1], (8, H)) * z[j]
                a[g] = new
    return jnp.concatenate(out, 0)

N = 2560
NB = N // B
RC = 128


def factor_kernel(g_hbm, r_ref, o_ref, panel, low, y_low, y, x_low, w_low, acc, sems):
    def fetch(k, slot):
        cols = pl.ds(pl.multiple_of(k * B, B), B)
        return pltpu.make_async_copy(g_hbm.at[:, cols], panel.at[slot], sems.at[slot])

    fetch(0, 0).start()
    row = lax.broadcasted_iota(jnp.int32, (B, B), 0)
    col = lax.broadcasted_iota(jnp.int32, (B, B), 1)

    def step(k, _):
        slot = lax.rem(k, 2)
        fetch(k, slot).wait()

        @pl.when(k + 1 < NB)
        def _():
            fetch(k + 1, 1 - slot).start()

        own_cols = pl.ds(pl.multiple_of(k * B, B), B)

        def subtract(lhs_ref, rows, acc_rows):
            def one(j, _):
                cols = pl.ds(pl.multiple_of(j * B, B), B)
                lhs = lhs_ref[:, cols]
                both = mm(lhs, low[k, :B, cols], NT)
                cross = mm(lhs[:rows], low[k, B:, cols], NT)
                acc[acc_rows, :] = acc[acc_rows, :] - (both[:rows] + (both[rows:] + cross))
                return 0

            lax.fori_loop(0, k, one, 0)

        tile = panel[slot, own_cols, :]
        acc[...] = jnp.where(row == col, tile, SHRINK * tile)
        subtract(low.at[k], B, pl.ds(0, B))
        w1 = inverse_factor(acc[:H, :H])
        l21 = mm3(acc[H:, :H], w1, NT)
        w2 = inverse_factor(acc[H:, H:] - mm3(l21, l21, NT))
        w21 = -mm3(w2, mm3(l21, w1))
        top = jnp.concatenate([w1, jnp.zeros((H, H), f32)], 1)
        w = jnp.concatenate([top, jnp.concatenate([w21, w2], 1)], 0)
        wh, wl = split(w)
        w_low[k, :B, :] = wh
        w_low[k, B:, :] = wl

        def scale(value):
            ch, cl = split(value)
            wh = w_low[k, :B, :]
            return mm(ch, wh, NT) + (mm(ch, w_low[k, B:, :], NT) + mm(cl, wh, NT))

        def below(i, _):
            acc[...] = SHRINK * panel[slot, pl.ds(pl.multiple_of(i * B, B), B), :]
            subtract(low.at[i], B, pl.ds(0, B))
            h, l = split(scale(acc[...]))
            low[i, :B, own_cols] = h
            low[i, B:, own_cols] = l
            return 0

        lax.fori_loop(k + 1, NB, below, 0)
        acc[:RC, :] = r_ref[:, own_cols]
        subtract(y_low, RC, pl.ds(0, RC))
        yk = scale(acc[:RC, :])
        y[:, own_cols] = yk
        h, l = split(yk)
        y_low[:RC, own_cols] = h
        y_low[RC:, own_cols] = l
        return 0

    lax.fori_loop(0, NB, step, 0)

    def back(s, _):
        k = NB - 1 - s
        own_cols = pl.ds(pl.multiple_of(k * B, B), B)
        acc[:RC, :] = y[:, own_cols]

        def one(i, _):
            cols = pl.ds(pl.multiple_of(i * B, B), B)
            lhs = x_low[:, cols]
            both = mm(lhs, low[i, :B, own_cols])
            cross = mm(lhs[:RC], low[i, B:, own_cols])
            acc[:RC, :] = acc[:RC, :] - (both[:RC] + (both[RC:] + cross))
            return 0

        lax.fori_loop(k + 1, NB, one, 0)
        ch, cl = split(acc[:RC, :])
        wh = w_low[k, :B, :]
        xk = mm(ch, wh) + (mm(ch, w_low[k, B:, :]) + mm(cl, wh))
        h, l = split(xk)
        x_low[:RC, own_cols] = h
        x_low[RC:, own_cols] = l
        o_ref[own_cols, :] = xk.T.astype(bf16)
        return 0

    lax.fori_loop(0, NB, back, 0)


def factor_solve(gram, right_t):
    return pl.pallas_call(
        factor_kernel,
        out_shape=jax.ShapeDtypeStruct((N, RC), bf16),
        in_specs=[pl.BlockSpec(memory_space=pl.ANY), pl.BlockSpec(memory_space=pltpu.VMEM)],
        out_specs=pl.BlockSpec(memory_space=pltpu.VMEM),
        scratch_shapes=[
            pltpu.VMEM((2, N, B), f32),
            pltpu.VMEM((NB, 2 * B, N), bf16),
            pltpu.VMEM((2 * RC, N), bf16),
            pltpu.VMEM((RC, N), f32),
            pltpu.VMEM((2 * RC, N), bf16),
            pltpu.VMEM((NB, 2 * B, B), bf16),
            pltpu.VMEM((B, B), f32),
            pltpu.SemaphoreType.DMA((2,)),
        ],
        compiler_params=pltpu.CompilerParams(vmem_limit_bytes=56 * 1024 * 1024),
    )(gram, right_t)


def local(acts, weights):
    own = acts[0]
    gathered = lax.all_gather(own, "tp", axis=1, tiled=True)
    columns = lax.all_to_all(weights[0], "tp", split_axis=1, concat_axis=0, tiled=True)
    projected = mm(gathered, columns).astype(bf16)
    diag = jnp.sum(jnp.square(gathered.astype(f32)), axis=0)
    right_t = SHRINK * mm(projected, gathered, TN)
    right_t = right_t + (1.0 - SHRINK) * diag[None, :] * columns.T.astype(f32)
    share = lax.psum_scatter(mm(own, gathered, TN), "member", scatter_dimension=0, tiled=True)
    gram = lax.all_gather(share, ("tp", "member"), axis=0, tiled=True)
    right_t = lax.psum(right_t, "member")
    return factor_solve(gram, right_t)


def solution(mesh):
    in_specs = (P("member", None, "tp"), P("member", "tp", None))
    return jax.shard_map(
        local, mesh=mesh, in_specs=in_specs, out_specs=P(None, "tp"), check_vma=False
    )
```

```python
import jax
import jax.numpy as jnp
from jax import lax
from jax.experimental import pallas as pl
from jax.experimental.pallas import tpu as pltpu
from jax.sharding import PartitionSpec as P

f32, bf16 = jnp.float32, jnp.bfloat16
SHRINK = 0.9
B = 256
H = 128
NT = (((1,), (1,)), ((), ()))
NN = (((1,), (0,)), ((), ()))


def split(x):
    hi = x.astype(bf16)
    return hi, (x - hi.astype(f32)).astype(bf16)


def mm(a, b, dims=NN):
    return lax.dot_general(a, b, dims, preferred_element_type=f32)


def mm3(a, b, dims=NN):
    ah, al = split(a)
    bh, bl = split(b)
    return mm(ah, bh, dims) + (mm(ah, bl, dims) + mm(al, bh, dims))


def recip(d):
    r = pl.reciprocal(d, approx=True)
    r = r * (2.0 - d * r)
    return r * (2.0 - d * r)


def inverse_factor(block):
    groups = H // 8
    lane = lax.broadcasted_iota(jnp.int32, (8, H), 1)
    sub = lax.broadcasted_iota(jnp.int32, (8, H), 0)
    a = [block[8 * g : 8 * g + 8, :] for g in range(groups)]
    out = []
    for t in range(groups):
        base = 8 * t
        slab = a[t]
        in_block = (lane >= base) & (lane < base + 8)
        rows = [jnp.broadcast_to(slab[i : i + 1, :], (8, H)) for i in range(8)]
        e = [
            [jnp.broadcast_to(rows[i][:, base + c : base + c + 1], (8, H)) for c in range(i + 1)]
            for i in range(8)
        ]
        r = [jnp.where(in_block, (lane == base + i).astype(f32), rows[i]) for i in range(8)]
        inv = [None] * 8
        low = [[None] * 8 for _ in range(8)]
        for c in range(8):
            inv[c] = recip(e[c][c])
            for i in range(c + 1, 8):
                low[i][c] = e[i][c] * inv[c]
            for i in range(c + 1, 8):
                for j in range(c + 1, i + 1):
                    e[i][j] = e[i][j] - low[i][c] * e[j][c]
                r[i] = r[i] - low[i][c] * r[c]
        own = jnp.zeros((8, H), f32)
        for i in range(8):
            own = jnp.where(sub == i, r[i] * lax.rsqrt(e[i][i]), own)
        out.append(jnp.where(lane < base + 8, own, 0.0))
        if t + 1 < groups:
            z = [r[i] * inv[i] for i in range(8)]
            for i in range(7, 0, -1):
                for j in range(i):
                    z[j] = z[j] - low[i][j] * z[i]
            for g in range(t + 1, groups):
                new = jnp.where(in_block, 0.0, a[g])
                for j in range(8):
                    new = new - jnp.broadcast_to(a[g][:, base + j : base + j + 1], (8, H)) * z[j]
                a[g] = new
    return jnp.concatenate(out, 0)

MESH = pl.DeviceIdType.MESH
TN = (((0,), (0,)), ((), ()))
NS = 7
PARTS = ((0, 2), (2, 2), (4, 3))


def place():
    m = lax.axis_index("member")
    t = lax.axis_index("tp")
    x = (t // 4) * 2 + (m // 2) % 2
    return x, m // 4, t % 4, m % 2


def device(x, y, z, c):
    return ((y * 2 + x % 2) * 2 + c, (x // 2) * 4 + z)


def greet(peers):
    barrier = pltpu.get_barrier_semaphore()
    for peer in peers:
        pl.semaphore_signal(barrier, inc=1, device_id=peer, device_id_type=MESH)
    pl.semaphore_wait(barrier, len(peers))


def remote(src, dst, send, recv, peer):
    return pltpu.make_async_remote_copy(
        src_ref=src, dst_ref=dst, send_sem=send, recv_sem=recv, device_id=peer, device_id_type=MESH
    )


def gather_kernel(a_ref, w_ref, at_ref, wc_ref, wx, send, recv, own):
    x, y, z, c = place()
    xh = x // 2
    t = xh * 4 + z
    other = (1 - xh) * 4 + z
    half = a_ref.shape[0] // 2
    partner = device((x + 2) % 4, y, z, c)
    ring = [device(x, y, (z + d) % 4, c) for d in range(4)]
    greet([partner] + ring[1:])

    def copy(i, src, dst, peer):
        made = remote(src, dst, send.at[i], recv.at[i], peer)
        made.start()
        return made

    def cols(first):
        return pl.ds(pl.multiple_of(first * 128, 128), 128)

    copies = {}
    copies[0] = copy(0, a_ref, at_ref.at[t], partner)
    copies[1] = copy(1, a_ref, at_ref.at[t], ring[1])
    copies[2] = copy(2, a_ref, at_ref.at[t], ring[3])
    far = pl.ds(pl.multiple_of((1 - xh) * 512, 512), 512)
    copies[9] = copy(9, w_ref.at[:, far], wx, partner)
    for d in range(1, 4):
        src = w_ref.at[:, cols(xh * 4 + (z + d) % 4)]
        copies[9 + d] = copy(9 + d, src, wc_ref.at[t], ring[d])
    keep_a = pltpu.make_async_copy(a_ref, at_ref.at[t], own.at[0])
    keep_a.start()
    keep_w = pltpu.make_async_copy(w_ref.at[:, cols(t)], wc_ref.at[t], own.at[1])
    keep_w.start()
    copies[0].wait_recv()
    copies[3] = copy(3, at_ref.at[other], at_ref.at[other], ring[1])
    copies[4] = copy(4, at_ref.at[other], at_ref.at[other], ring[3])
    for at, side in ((0, xh), (2, 1 - xh)):
        before = side * 4 + (z + 3) % 4
        after = side * 4 + (z + 1) % 4
        copies[1 + at].wait_recv()
        part = at_ref.at[before, pl.ds(0, half)]
        copies[5 + at] = copy(5 + at, part, part, ring[1])
        copies[2 + at].wait_recv()
        part = at_ref.at[after, pl.ds(half, half)]
        copies[6 + at] = copy(6 + at, part, part, ring[3])
    copies[9].wait_recv()
    keep_x = pltpu.make_async_copy(wx.at[:, cols(z)], wc_ref.at[other], own.at[2])
    keep_x.start()
    for d in range(1, 4):
        src = wx.at[:, cols((z + d) % 4)]
        copies[12 + d] = copy(12 + d, src, wc_ref.at[other], ring[d])
    for i in (5, 6, 7, 8, 10, 11, 12, 13, 14, 15):
        copies[i].wait_recv()
    for i in range(16):
        copies[i].wait_send()
    keep_a.wait()
    keep_w.wait()
    keep_x.wait()


def gather_acts(acts_t, weight):
    width, rows = acts_t.shape
    vmem = pl.BlockSpec(memory_space=pltpu.VMEM)
    return pl.pallas_call(
        gather_kernel,
        out_shape=(
            jax.ShapeDtypeStruct((8, width, rows), bf16),
            jax.ShapeDtypeStruct((8, width, 128), bf16),
        ),
        in_specs=[vmem, vmem],
        out_specs=(vmem, vmem),
        scratch_shapes=[
            pltpu.VMEM((width, 512), bf16),
            pltpu.SemaphoreType.DMA((16,)),
            pltpu.SemaphoreType.DMA((16,)),
            pltpu.SemaphoreType.DMA((3,)),
        ],
        compiler_params=pltpu.CompilerParams(
            collective_id=0, has_side_effects=True, vmem_limit_bytes=32 * 1024 * 1024
        ),
    )(acts_t, weight)


def product_kernel(at_ref, wc_ref, part_ref, right_ref):
    t = lax.axis_index("tp")
    projected = mm(at_ref[...], wc_ref[...], TN).astype(bf16)
    for i in range(10):
        rows = pl.ds(i * 256, 256)
        own = at_ref[rows, :]
        wide = own.astype(f32)
        diag = jnp.sum(wide * wide, axis=1, keepdims=True)
        scaled = diag * wc_ref[rows, :].astype(f32)
        right_ref[rows, :] = SHRINK * mm(own, projected) + (1.0 - SHRINK) * scaled
    for s in range(NS):
        b = jnp.minimum(s * 8 + t, 54)
        k = 0
        for j in range(1, 10):
            k = k + (b >= 10 * j - j * (j - 1) // 2).astype(jnp.int32)
        i = b - (10 * k - k * (k - 1) // 2) + k
        left = at_ref[pl.ds(pl.multiple_of(i * 256, 256), 256), :]
        right = at_ref[pl.ds(pl.multiple_of(k * 256, 256), 256), :]
        part_ref[s] = mm(left, right, NT)


def products(at, wc):
    vmem = pl.BlockSpec(memory_space=pltpu.VMEM)
    return pl.pallas_call(
        product_kernel,
        out_shape=(
            jax.ShapeDtypeStruct((NS, 256, 256), f32),
            jax.ShapeDtypeStruct((2560, 128), f32),
        ),
        in_specs=[vmem, vmem],
        out_specs=(vmem, vmem),
        compiler_params=pltpu.CompilerParams(vmem_limit_bytes=40 * 1024 * 1024),
    )(at, wc)


def sum_kernel(g_ref, r_ref, go_ref, ro_ref, g_pair, r_pair, g_in, r_in, send, recv):
    x, y, z, c = place()
    q = (x % 2) * 4 + y
    pair = device(x, y, z, 1 - c)
    peers = []
    for d in range(1, 8):
        p = (q + d) % 8
        peers.append((p, device((x // 2) * 2 + p // 4, p % 4, z, c)))
    greet([pair] + [device_id for _, device_id in peers])
    first = [
        remote(g_ref.at[:, 1 - c], g_pair, send.at[0], recv.at[0], pair),
        remote(r_ref.at[1 - c], r_pair, send.at[1], recv.at[1], pair),
    ]
    for copy in first:
        copy.start()
    for copy in first:
        copy.wait_recv()
    g_pair[...] = g_pair[...] + g_ref[:, c]
    r_pair[...] = r_pair[...] + r_ref[c]
    second = []
    for d, (p, peer) in enumerate(peers):
        second.append(remote(g_pair.at[:, p], g_in.at[d], send.at[2 + d], recv.at[2 + d], peer))
        second.append(remote(r_pair.at[p], r_in.at[d], send.at[9 + d], recv.at[9 + d], peer))
    for copy in second:
        copy.start()
    for copy in second:
        copy.wait_recv()
    g_sum = g_pair[:, q]
    r_sum = r_pair[q]
    for d in range(7):
        g_sum = g_sum + g_in[d]
        r_sum = r_sum + r_in[d]
    go_ref[...] = g_sum
    ro_ref[...] = r_sum
    for copy in first + second:
        copy.wait_send()


def sum_members(part, right):
    vmem = pl.BlockSpec(memory_space=pltpu.VMEM)
    return pl.pallas_call(
        sum_kernel,
        out_shape=(
            jax.ShapeDtypeStruct((NS, 16, 256), f32),
            jax.ShapeDtypeStruct((160, 128), f32),
        ),
        in_specs=[vmem, vmem],
        out_specs=(vmem, vmem),
        scratch_shapes=[
            pltpu.VMEM((NS, 8, 16, 256), f32),
            pltpu.VMEM((8, 160, 128), f32),
            pltpu.VMEM((7, NS, 16, 256), f32),
            pltpu.VMEM((7, 160, 128), f32),
            pltpu.SemaphoreType.DMA((16,)),
            pltpu.SemaphoreType.DMA((16,)),
        ],
        compiler_params=pltpu.CompilerParams(
            collective_id=1, has_side_effects=True, vmem_limit_bytes=40 * 1024 * 1024
        ),
    )(part.reshape(NS, 2, 8, 16, 256), right.reshape(2, 8, 160, 128))


def spread_kernel(g_ref, r_ref, go_ref, ro_ref, send, recv, rsend, rrecv, own):
    x, y, z, c = place()
    coord = (x, y, z)
    q = (x % 2) * 4 + y
    pair = device(x, y, z, 1 - c)
    peers = []
    for d in range(1, 8):
        p = (q + d) % 8
        peers.append(device((x // 2) * 2 + p // 4, p % 4, z, c))

    def along(axis, shift):
        moved = list(coord)
        moved[axis] = (moved[axis] + shift) % 4
        return device(*moved, c)

    ring = [(along(axis, 1), along(axis, 3)) for axis in range(3)]
    greet([pair] + peers + [one for both in ring for one in both])

    keep_g = pltpu.make_async_copy(g_ref, go_ref.at[:, c, x, y, z], own.at[0])
    keep_r = pltpu.make_async_copy(r_ref, ro_ref.at[c * 8 + q], own.at[1])
    keep_g.start()
    keep_r.start()
    keep_g.wait()
    keep_r.wait()

    def view(p, phase, value, rows=None):
        order = (p, (p + 1) % 3, (p + 2) % 3)
        index = list(coord)
        for axis in order[:phase]:
            index[axis] = pl.ds(0, 4)
        index[order[phase]] = value
        first, count = PARTS[p]
        index = [pl.ds(first, count), c] + index
        if rows is not None:
            index.append(pl.ds(rows, 8))
        return go_ref.at[tuple(index)]

    started = []

    def copy(ref, sems, i, peer):
        made = remote(ref, ref, sems[0].at[i], sems[1].at[i], peer)
        made.start()
        started.append(made)
        return made

    g_sems, r_sems = (send, recv), (rsend, rrecv)
    r_copies = [copy(ro_ref.at[c * 8 + q], r_sems, d, peer) for d, peer in enumerate(peers)]
    last = []
    for phase in range(3):
        first = {}
        second = {}
        for p in range(3):
            axis = (p + phase) % 3
            mine = view(p, phase, coord[axis])
            base = (p * 3 + phase) * 4
            first[p] = (copy(mine, g_sems, base, ring[axis][0]), copy(mine, g_sems, base + 1, ring[axis][1]))
            if phase == 2:
                last.append(copy(mine, g_sems, 36 + p * 4, pair))
        for p in range(3):
            axis = (p + phase) % 3
            base = (p * 3 + phase) * 4
            before, after = (coord[axis] + 3) % 4, (coord[axis] + 1) % 4
            first[p][0].wait_recv()
            one = copy(view(p, phase, before, 0), g_sems, base + 2, ring[axis][0])
            first[p][1].wait_recv()
            two = copy(view(p, phase, after, 8), g_sems, base + 3, ring[axis][1])
            second[p] = (one, two)
            if phase == 2:
                last.append(copy(view(p, phase, before), g_sems, 37 + p * 4, pair))
                last.append(copy(view(p, phase, after), g_sems, 38 + p * 4, pair))
        if phase == 0:
            for made in r_copies:
                made.wait_recv()
            last.append(copy(ro_ref.at[pl.ds(pl.multiple_of(c * 8, 8), 8)], r_sems, 7, pair))
        for p in range(3):
            axis = (p + phase) % 3
            second[p][0].wait_recv()
            second[p][1].wait_recv()
            if phase == 2:
                far = (coord[axis] + 2) % 4
                last.append(copy(view(p, phase, far), g_sems, 39 + p * 4, pair))
    for made in last:
        made.wait_recv()
    for made in started:
        made.wait_send()


def spread(gram, right):
    hbm = pl.BlockSpec(memory_space=pl.ANY)
    vmem = pl.BlockSpec(memory_space=pltpu.VMEM)
    return pl.pallas_call(
        spread_kernel,
        out_shape=(
            jax.ShapeDtypeStruct((NS, 2, 4, 4, 4, 16, 256), f32),
            jax.ShapeDtypeStruct((16, 160, 128), f32),
        ),
        in_specs=[vmem, vmem],
        out_specs=(hbm, hbm),
        scratch_shapes=[
            pltpu.SemaphoreType.DMA((48,)),
            pltpu.SemaphoreType.DMA((48,)),
            pltpu.SemaphoreType.DMA((8,)),
            pltpu.SemaphoreType.DMA((8,)),
            pltpu.SemaphoreType.DMA((2,)),
        ],
        compiler_params=pltpu.CompilerParams(collective_id=2, has_side_effects=True),
    )(gram, right)

N = 2560
NB = N // B
RC = 128


def factor_kernel(g_hbm, r_ref, o_ref, panel, low, y_low, y, x_low, w_low, acc, sems):
    def block(k, i, slot):
        b = 10 * k - k * (k - 1) // 2 + i - k
        s, t = b // 8, b % 8
        src = g_hbm.at[s, :, pl.ds((t // 4) * 2, 2), :, t % 4]
        return pltpu.make_async_copy(src, panel.at[slot, i], sems.at[slot, i])

    def fetch(k, slot):
        def one(i, _):
            block(k, i, slot).start()
            return 0

        lax.fori_loop(k, NB, one, 0)

    fetch(0, 0)
    row = lax.broadcasted_iota(jnp.int32, (B, B), 0)
    col = lax.broadcasted_iota(jnp.int32, (B, B), 1)

    def step(k, _):
        slot = k % 2
        block(k, k, slot).wait()

        @pl.when(k + 1 < NB)
        def _():
            fetch(k + 1, 1 - slot)

        own_cols = pl.ds(pl.multiple_of(k * B, B), B)

        def subtract(lhs_ref, rows, acc_rows):
            def one(j, _):
                cols = pl.ds(pl.multiple_of(j * B, B), B)
                lhs = lhs_ref[:, cols]
                both = mm(lhs, low[k, :B, cols], NT)
                cross = mm(lhs[:rows], low[k, B:, cols], NT)
                acc[acc_rows, :] = acc[acc_rows, :] - (both[:rows] + (both[rows:] + cross))
                return 0

            lax.fori_loop(0, k, one, 0)

        tile = panel[slot, k].reshape(B, B)
        acc[...] = jnp.where(row == col, tile, SHRINK * tile)
        subtract(low.at[k], B, pl.ds(0, B))
        w1 = inverse_factor(acc[:H, :H])
        l21 = mm3(acc[H:, :H], w1, NT)
        w2 = inverse_factor(acc[H:, H:] - mm3(l21, l21, NT))
        w21 = -mm3(w2, mm3(l21, w1))
        top = jnp.concatenate([w1, jnp.zeros((H, H), f32)], 1)
        w = jnp.concatenate([top, jnp.concatenate([w21, w2], 1)], 0)
        wh, wl = split(w)
        w_low[k, :B, :] = wh
        w_low[k, B:, :] = wl

        def scale(value):
            ch, cl = split(value)
            wh = w_low[k, :B, :]
            return mm(ch, wh, NT) + (mm(ch, w_low[k, B:, :], NT) + mm(cl, wh, NT))

        def below(i, _):
            block(k, i, slot).wait()
            acc[...] = SHRINK * panel[slot, i].reshape(B, B)
            subtract(low.at[i], B, pl.ds(0, B))
            h, l = split(scale(acc[...]))
            low[i, :B, own_cols] = h
            low[i, B:, own_cols] = l
            return 0

        lax.fori_loop(k + 1, NB, below, 0)
        acc[:RC, :] = r_ref[own_cols, :].T
        subtract(y_low, RC, pl.ds(0, RC))
        yk = scale(acc[:RC, :])
        y[:, own_cols] = yk
        h, l = split(yk)
        y_low[:RC, own_cols] = h
        y_low[RC:, own_cols] = l
        return 0

    lax.fori_loop(0, NB, step, 0)

    def back(s, _):
        k = NB - 1 - s
        own_cols = pl.ds(pl.multiple_of(k * B, B), B)
        acc[:RC, :] = y[:, own_cols]

        def one(i, _):
            cols = pl.ds(pl.multiple_of(i * B, B), B)
            lhs = x_low[:, cols]
            both = mm(lhs, low[i, :B, own_cols])
            cross = mm(lhs[:RC], low[i, B:, own_cols])
            acc[:RC, :] = acc[:RC, :] - (both[:RC] + (both[RC:] + cross))
            return 0

        lax.fori_loop(k + 1, NB, one, 0)
        ch, cl = split(acc[:RC, :])
        wh = w_low[k, :B, :]
        xk = mm(ch, wh) + (mm(ch, w_low[k, B:, :]) + mm(cl, wh))
        h, l = split(xk)
        x_low[:RC, own_cols] = h
        x_low[RC:, own_cols] = l
        o_ref[own_cols, :] = xk.T.astype(bf16)
        return 0

    lax.fori_loop(0, NB, back, 0)


def factor_solve(gram, right):
    return pl.pallas_call(
        factor_kernel,
        out_shape=jax.ShapeDtypeStruct((N, RC), bf16),
        in_specs=[pl.BlockSpec(memory_space=pl.ANY), pl.BlockSpec(memory_space=pltpu.VMEM)],
        out_specs=pl.BlockSpec(memory_space=pltpu.VMEM),
        scratch_shapes=[
            pltpu.VMEM((2, NB, 2, 2, 4, 16, 256), f32),
            pltpu.VMEM((NB, 2 * B, N), bf16),
            pltpu.VMEM((2 * RC, N), bf16),
            pltpu.VMEM((RC, N), f32),
            pltpu.VMEM((2 * RC, N), bf16),
            pltpu.VMEM((NB, 2 * B, B), bf16),
            pltpu.VMEM((B, B), f32),
            pltpu.SemaphoreType.DMA((2, NB)),
        ],
        compiler_params=pltpu.CompilerParams(vmem_limit_bytes=56 * 1024 * 1024),
    )(gram, right)


def local(acts, weights):
    at, wc = gather_acts(acts[0].T, weights[0])
    part, right = products(at.reshape(N, -1), wc.reshape(N, RC))
    gram, right = spread(*sum_members(part, right))
    return factor_solve(gram, right.reshape(N, RC))


def solution(mesh):
    in_specs = (P("member", None, "tp"), P("member", "tp", None))
    return jax.shard_map(
        local, mesh=mesh, in_specs=in_specs, out_specs=P(None, "tp"), check_vma=False
    )
```

```python
import jax
import jax.numpy as jnp
from jax import lax
from jax.experimental import pallas as pl
from jax.experimental.pallas import tpu as pltpu
from jax.sharding import PartitionSpec as P

f32, bf16 = jnp.float32, jnp.bfloat16
SHRINK = 0.9
B = 256
H = 128
NT = (((1,), (1,)), ((), ()))
NN = (((1,), (0,)), ((), ()))


def split(x):
    hi = x.astype(bf16)
    return hi, (x - hi.astype(f32)).astype(bf16)


def mm(a, b, dims=NN):
    return lax.dot_general(a, b, dims, preferred_element_type=f32)


def mm3(a, b, dims=NN):
    ah, al = split(a)
    bh, bl = split(b)
    return mm(ah, bh, dims) + (mm(ah, bl, dims) + mm(al, bh, dims))


def tree_sum(terms):
    while len(terms) > 1:
        pairs = [terms[i] + terms[i + 1] for i in range(0, len(terms) - 1, 2)]
        terms = pairs + terms[len(pairs) * 2 :]
    return terms[0]


def inverse_factor(block):
    groups = H // 8
    lane = lax.broadcasted_iota(jnp.int32, (8, H), 1)
    sub = lax.broadcasted_iota(jnp.int32, (8, H), 0)
    a = [block[8 * g : 8 * g + 8, :] for g in range(groups)]
    out = []
    for t in range(groups):
        base = 8 * t
        slab = a[t]
        in_block = (lane >= base) & (lane < base + 8)
        rows = [jnp.broadcast_to(slab[i : i + 1, :], (8, H)) for i in range(8)]
        e = [
            [jnp.broadcast_to(rows[i][:, base + c : base + c + 1], (8, H)) for c in range(i + 1)]
            for i in range(8)
        ]
        r = [jnp.where(in_block, (lane == base + i).astype(f32), rows[i]) for i in range(8)]
        inv = [None] * 8
        piv = [None] * 8
        low = [[None] * 8 for _ in range(8)]
        unit = [[None] * 8 for _ in range(8)]

        def eliminate(c, i):
            r[i] = r[i] - low[i][c] * r[c]
            for j in range(c):
                unit[i][j] = unit[i][j] - low[i][c] * unit[c][j]
            unit[i][c] = -low[i][c]

        for c in range(0, 8, 2):
            d = c + 1
            p, q, s = e[c][c], e[d][c], e[d][d]
            det = p * s - q * q
            inv_p = pl.reciprocal(p, approx=True)
            inv_det = pl.reciprocal(det, approx=True)
            inv[c], inv[d] = inv_p, p * inv_det
            piv[c], piv[d] = p, det * inv_p
            low[d][c] = q * inv_p
            left = {i: e[i][c] * s - e[i][d] * q for i in range(c + 2, 8)}
            right = {i: e[i][d] * p - e[i][c] * q for i in range(c + 2, 8)}
            for i in range(c + 2, 8):
                for j in range(c + 2, i + 1):
                    e[i][j] = e[i][j] - (left[i] * e[j][c] + right[i] * e[j][d]) * inv_det
                low[i][c] = e[i][c] * inv_p
                low[i][d] = right[i] * inv_det
            eliminate(c, d)
            for i in range(c + 2, 8):
                eliminate(c, i)
                eliminate(d, i)
        own = jnp.zeros((8, H), f32)
        for i in range(8):
            own = jnp.where(sub == i, r[i] * lax.rsqrt(piv[i]), own)
        out.append(jnp.where(lane < base + 8, own, 0.0))
        if t + 1 < groups:
            v = [r[i] * inv[i] for i in range(8)]
            z = [tree_sum([v[j]] + [unit[i][j] * v[i] for i in range(j + 1, 8)]) for j in range(8)]
            for g in range(t + 1, groups):
                old = a[g]
                column = [jnp.broadcast_to(old[:, base + j : base + j + 1], (8, H)) for j in range(8)]
                a[g] = jnp.where(in_block, 0.0, old) - tree_sum([column[j] * z[j] for j in range(8)])
    return jnp.concatenate(out, 0)

MESH = pl.DeviceIdType.MESH
TN = (((0,), (0,)), ((), ()))
NS = 7
PARTS = ((0, 2), (2, 2), (4, 3))


def place():
    m = lax.axis_index("member")
    t = lax.axis_index("tp")
    x = (t // 4) * 2 + (m // 2) % 2
    return x, m // 4, t % 4, m % 2


def device(x, y, z, c):
    return ((y * 2 + x % 2) * 2 + c, (x // 2) * 4 + z)


def greet(peers):
    barrier = pltpu.get_barrier_semaphore()
    for peer in peers:
        pl.semaphore_signal(barrier, inc=1, device_id=peer, device_id_type=MESH)
    pl.semaphore_wait(barrier, len(peers))


def remote(src, dst, send, recv, peer):
    return pltpu.make_async_remote_copy(
        src_ref=src, dst_ref=dst, send_sem=send, recv_sem=recv, device_id=peer, device_id_type=MESH
    )


def gather_kernel(a_ref, w_ref, at_ref, wc_ref, wx, send, recv, own):
    x, y, z, c = place()
    xh = x // 2
    t = xh * 4 + z
    other = (1 - xh) * 4 + z
    half = a_ref.shape[0] // 2
    partner = device((x + 2) % 4, y, z, c)
    ring = [device(x, y, (z + d) % 4, c) for d in range(4)]
    greet([partner] + ring[1:])

    def copy(i, src, dst, peer):
        made = remote(src, dst, send.at[i], recv.at[i], peer)
        made.start()
        return made

    def cols(first):
        return pl.ds(pl.multiple_of(first * 128, 128), 128)

    copies = {}
    copies[0] = copy(0, a_ref, at_ref.at[t], partner)
    copies[1] = copy(1, a_ref, at_ref.at[t], ring[1])
    copies[2] = copy(2, a_ref, at_ref.at[t], ring[3])
    far = pl.ds(pl.multiple_of((1 - xh) * 512, 512), 512)
    copies[9] = copy(9, w_ref.at[:, far], wx, partner)
    for d in range(1, 4):
        src = w_ref.at[:, cols(xh * 4 + (z + d) % 4)]
        copies[9 + d] = copy(9 + d, src, wc_ref.at[t], ring[d])
    keep_a = pltpu.make_async_copy(a_ref, at_ref.at[t], own.at[0])
    keep_a.start()
    keep_w = pltpu.make_async_copy(w_ref.at[:, cols(t)], wc_ref.at[t], own.at[1])
    keep_w.start()
    copies[0].wait_recv()
    copies[3] = copy(3, at_ref.at[other], at_ref.at[other], ring[1])
    copies[4] = copy(4, at_ref.at[other], at_ref.at[other], ring[3])
    for at, side in ((0, xh), (2, 1 - xh)):
        before = side * 4 + (z + 3) % 4
        after = side * 4 + (z + 1) % 4
        copies[1 + at].wait_recv()
        part = at_ref.at[before, pl.ds(0, half)]
        copies[5 + at] = copy(5 + at, part, part, ring[1])
        copies[2 + at].wait_recv()
        part = at_ref.at[after, pl.ds(half, half)]
        copies[6 + at] = copy(6 + at, part, part, ring[3])
    copies[9].wait_recv()
    keep_x = pltpu.make_async_copy(wx.at[:, cols(z)], wc_ref.at[other], own.at[2])
    keep_x.start()
    for d in range(1, 4):
        src = wx.at[:, cols((z + d) % 4)]
        copies[12 + d] = copy(12 + d, src, wc_ref.at[other], ring[d])
    for i in (5, 6, 7, 8, 10, 11, 12, 13, 14, 15):
        copies[i].wait_recv()
    for i in range(16):
        copies[i].wait_send()
    keep_a.wait()
    keep_w.wait()
    keep_x.wait()


def gather_acts(acts_t, weight):
    width, rows = acts_t.shape
    vmem = pl.BlockSpec(memory_space=pltpu.VMEM)
    return pl.pallas_call(
        gather_kernel,
        out_shape=(
            jax.ShapeDtypeStruct((8, width, rows), bf16),
            jax.ShapeDtypeStruct((8, width, 128), bf16),
        ),
        in_specs=[vmem, vmem],
        out_specs=(vmem, vmem),
        scratch_shapes=[
            pltpu.VMEM((width, 512), bf16),
            pltpu.SemaphoreType.DMA((16,)),
            pltpu.SemaphoreType.DMA((16,)),
            pltpu.SemaphoreType.DMA((3,)),
        ],
        compiler_params=pltpu.CompilerParams(
            collective_id=0, has_side_effects=True, vmem_limit_bytes=32 * 1024 * 1024
        ),
    )(acts_t, weight)


def product_kernel(at_ref, wc_ref, part_ref, right_ref):
    t = lax.axis_index("tp")
    projected = mm(at_ref[...], wc_ref[...], TN).astype(bf16)
    for i in range(10):
        rows = pl.ds(i * 256, 256)
        own = at_ref[rows, :]
        wide = own.astype(f32)
        diag = jnp.sum(wide * wide, axis=1, keepdims=True)
        scaled = diag * wc_ref[rows, :].astype(f32)
        right_ref[rows, :] = SHRINK * mm(own, projected) + (1.0 - SHRINK) * scaled
    for s in range(NS):
        b = jnp.minimum(s * 8 + t, 54)
        k = 0
        for j in range(1, 10):
            k = k + (b >= 10 * j - j * (j - 1) // 2).astype(jnp.int32)
        i = b - (10 * k - k * (k - 1) // 2) + k
        left = at_ref[pl.ds(pl.multiple_of(i * 256, 256), 256), :]
        right = at_ref[pl.ds(pl.multiple_of(k * 256, 256), 256), :]
        part_ref[s] = mm(left, right, NT)


def products(at, wc):
    vmem = pl.BlockSpec(memory_space=pltpu.VMEM)
    return pl.pallas_call(
        product_kernel,
        out_shape=(
            jax.ShapeDtypeStruct((NS, 256, 256), f32),
            jax.ShapeDtypeStruct((2560, 128), f32),
        ),
        in_specs=[vmem, vmem],
        out_specs=(vmem, vmem),
        compiler_params=pltpu.CompilerParams(vmem_limit_bytes=40 * 1024 * 1024),
    )(at, wc)


def sum_kernel(g_ref, r_ref, go_ref, ro_ref, g_pair, r_pair, g_in, r_in, send, recv):
    x, y, z, c = place()
    q = (x % 2) * 4 + y
    pair = device(x, y, z, 1 - c)
    peers = []
    for d in range(1, 8):
        p = (q + d) % 8
        peers.append((p, device((x // 2) * 2 + p // 4, p % 4, z, c)))
    greet([pair] + [device_id for _, device_id in peers])
    first = [
        remote(g_ref.at[:, 1 - c], g_pair, send.at[0], recv.at[0], pair),
        remote(r_ref.at[1 - c], r_pair, send.at[1], recv.at[1], pair),
    ]
    for copy in first:
        copy.start()
    for copy in first:
        copy.wait_recv()
    g_pair[...] = g_pair[...] + g_ref[:, c]
    r_pair[...] = r_pair[...] + r_ref[c]
    second = []
    for d, (p, peer) in enumerate(peers):
        second.append(remote(g_pair.at[:, p], g_in.at[d], send.at[2 + d], recv.at[2 + d], peer))
        second.append(remote(r_pair.at[p], r_in.at[d], send.at[9 + d], recv.at[9 + d], peer))
    for copy in second:
        copy.start()
    for copy in second:
        copy.wait_recv()
    g_sum = g_pair[:, q]
    r_sum = r_pair[q]
    for d in range(7):
        g_sum = g_sum + g_in[d]
        r_sum = r_sum + r_in[d]
    go_ref[...] = g_sum
    ro_ref[...] = r_sum
    for copy in first + second:
        copy.wait_send()


def sum_members(part, right):
    vmem = pl.BlockSpec(memory_space=pltpu.VMEM)
    return pl.pallas_call(
        sum_kernel,
        out_shape=(
            jax.ShapeDtypeStruct((NS, 16, 256), f32),
            jax.ShapeDtypeStruct((160, 128), f32),
        ),
        in_specs=[vmem, vmem],
        out_specs=(vmem, vmem),
        scratch_shapes=[
            pltpu.VMEM((NS, 8, 16, 256), f32),
            pltpu.VMEM((8, 160, 128), f32),
            pltpu.VMEM((7, NS, 16, 256), f32),
            pltpu.VMEM((7, 160, 128), f32),
            pltpu.SemaphoreType.DMA((16,)),
            pltpu.SemaphoreType.DMA((16,)),
        ],
        compiler_params=pltpu.CompilerParams(
            collective_id=1, has_side_effects=True, vmem_limit_bytes=40 * 1024 * 1024
        ),
    )(part.reshape(NS, 2, 8, 16, 256), right.reshape(2, 8, 160, 128))


def spread_kernel(g_ref, r_ref, go_ref, ro_ref, send, recv, rsend, rrecv, own):
    x, y, z, c = place()
    coord = (x, y, z)
    q = (x % 2) * 4 + y
    pair = device(x, y, z, 1 - c)
    peers = []
    for d in range(1, 8):
        p = (q + d) % 8
        peers.append(device((x // 2) * 2 + p // 4, p % 4, z, c))

    def along(axis, shift):
        moved = list(coord)
        moved[axis] = (moved[axis] + shift) % 4
        return device(*moved, c)

    ring = [(along(axis, 1), along(axis, 3)) for axis in range(3)]
    greet([pair] + peers + [one for both in ring for one in both])

    keep_g = pltpu.make_async_copy(g_ref, go_ref.at[:, c, x, y, z], own.at[0])
    keep_r = pltpu.make_async_copy(r_ref, ro_ref.at[c * 8 + q], own.at[1])
    keep_g.start()
    keep_r.start()
    keep_g.wait()
    keep_r.wait()

    def view(p, phase, value, rows=None):
        order = (p, (p + 1) % 3, (p + 2) % 3)
        index = list(coord)
        for axis in order[:phase]:
            index[axis] = pl.ds(0, 4)
        index[order[phase]] = value
        first, count = PARTS[p]
        index = [pl.ds(first, count), c] + index
        if rows is not None:
            index.append(pl.ds(rows, 8))
        return go_ref.at[tuple(index)]

    started = []

    def copy(ref, sems, i, peer):
        made = remote(ref, ref, sems[0].at[i], sems[1].at[i], peer)
        made.start()
        started.append(made)
        return made

    g_sems, r_sems = (send, recv), (rsend, rrecv)
    r_copies = [copy(ro_ref.at[c * 8 + q], r_sems, d, peer) for d, peer in enumerate(peers)]
    last = []
    for phase in range(3):
        first = {}
        second = {}
        for p in range(3):
            axis = (p + phase) % 3
            mine = view(p, phase, coord[axis])
            base = (p * 3 + phase) * 4
            first[p] = (copy(mine, g_sems, base, ring[axis][0]), copy(mine, g_sems, base + 1, ring[axis][1]))
            if phase == 2:
                last.append(copy(mine, g_sems, 36 + p * 4, pair))
        for p in range(3):
            axis = (p + phase) % 3
            base = (p * 3 + phase) * 4
            before, after = (coord[axis] + 3) % 4, (coord[axis] + 1) % 4
            first[p][0].wait_recv()
            one = copy(view(p, phase, before, 0), g_sems, base + 2, ring[axis][0])
            first[p][1].wait_recv()
            two = copy(view(p, phase, after, 8), g_sems, base + 3, ring[axis][1])
            second[p] = (one, two)
            if phase == 2:
                last.append(copy(view(p, phase, before), g_sems, 37 + p * 4, pair))
                last.append(copy(view(p, phase, after), g_sems, 38 + p * 4, pair))
        if phase == 0:
            for made in r_copies:
                made.wait_recv()
            last.append(copy(ro_ref.at[pl.ds(pl.multiple_of(c * 8, 8), 8)], r_sems, 7, pair))
        for p in range(3):
            axis = (p + phase) % 3
            second[p][0].wait_recv()
            second[p][1].wait_recv()
            if phase == 2:
                far = (coord[axis] + 2) % 4
                last.append(copy(view(p, phase, far), g_sems, 39 + p * 4, pair))
    for made in last:
        made.wait_recv()
    for made in started:
        made.wait_send()


def spread(gram, right):
    hbm = pl.BlockSpec(memory_space=pl.ANY)
    vmem = pl.BlockSpec(memory_space=pltpu.VMEM)
    return pl.pallas_call(
        spread_kernel,
        out_shape=(
            jax.ShapeDtypeStruct((NS, 2, 4, 4, 4, 16, 256), f32),
            jax.ShapeDtypeStruct((16, 160, 128), f32),
        ),
        in_specs=[vmem, vmem],
        out_specs=(hbm, hbm),
        scratch_shapes=[
            pltpu.SemaphoreType.DMA((48,)),
            pltpu.SemaphoreType.DMA((48,)),
            pltpu.SemaphoreType.DMA((8,)),
            pltpu.SemaphoreType.DMA((8,)),
            pltpu.SemaphoreType.DMA((2,)),
        ],
        compiler_params=pltpu.CompilerParams(collective_id=2, has_side_effects=True),
    )(gram, right)

N = 2560
NB = N // B
RC = 128
CLASSES = ((0, 3, 9), (3, 6, 6), (6, 10, 3))


def cut(k, width=B):
    return slice(k * B, k * B + width)


def prod(left, right, dims):
    lh, ll = left
    rh, rl = right
    return mm(lh, rh, dims) + (mm(ll, rh, dims) + mm(lh, rl, dims))


def factor_kernel(g_hbm, r_ref, o_ref, g, low, y_low, y, w_low, diag, panel, y_panel, sems):
    row = lax.broadcasted_iota(jnp.int32, (B, B), 0)
    col = lax.broadcasted_iota(jnp.int32, (B, B), 1)

    copies = [pltpu.make_async_copy(g_hbm.at[s], g.at[s], sems.at[s]) for s in range(NS)]
    for copy in copies:
        copy.start()

    def lanes(k):
        return pl.ds(pl.multiple_of(k * B, B), B)

    def gram(i, k):
        b = jnp.minimum(10 * k - k * (k - 1) // 2 + i - k, 54)
        s, t = b // 8, b % 8
        tile = g[s, :, pl.ds((t // 4) * 2, 2), :, t % 4].reshape(B, B)
        return tile

    def gram_diag(k):
        tile = gram(k, k)
        return jnp.where(row == col, tile, SHRINK * tile)

    def rows_of(i, width):
        return low[i, :B, :width], low[i, B:, :width]

    def put(i, k, value):
        h, l = split(value)
        low[i, :B, lanes(k)] = h
        low[i, B:, lanes(k)] = l

    def put_y(k, value):
        y[:, lanes(k)] = value
        if isinstance(k, int) and k == NB - 1:
            return
        h, l = split(value)
        y_low[:RC, lanes(k)] = h
        y_low[RC:, lanes(k)] = l

    def w_of(k):
        return w_low[k, :B, :], w_low[k, B:, :]

    def step(k, width, tiles):
        block = diag[...]
        w1 = inverse_factor(block[:H, :H])
        old, now = (k + 1) % 2, k % 2
        last = jnp.maximum(k - 1, 0)
        targets = [jnp.minimum(k + 1 + r, NB) for r in range(tiles)]
        w_old = w_of(last)
        for i in targets:
            put(i, last, prod(split(panel[old, i]), w_old, NT))
        put_y(last, prod(split(y_panel[old]), w_old, NT))
        w1s = split(w1)
        l21 = prod(split(block[H:, :H]), w1s, NT)
        l21s = split(l21)
        w2 = inverse_factor(block[H:, H:] - prod(l21s, l21s, NT))
        here = rows_of(k, width)
        for i in targets:
            panel[now, i] = SHRINK * gram(i, k) - prod(rows_of(i, width), here, NT)
        y_rows = y_low[:RC, :width], y_low[RC:, :width]
        y_panel[now] = r_ref[lanes(k), :].T - prod(y_rows, here, NT)
        low1 = prod(l21s, w1s, NN)
        mine = rows_of(k + 1, width)
        after = gram_diag(k + 1) - prod(mine, mine, NT)
        value = panel[now, k + 1]
        a1 = prod(split(value[:, :H]), w1s, NT)
        a1s = split(a1)
        after = after - prod(a1s, a1s, NT)
        rest = value[:, H:] - prod(a1s, l21s, NT)
        w2s = split(w2)
        a2s = split(prod(split(rest), w2s, NT))
        diag[...] = after - prod(a2s, a2s, NT)
        own = lanes(jnp.minimum(k, NB - 2))
        low[k + 1, :B, own] = jnp.concatenate([a1s[0], a2s[0]], 1)
        low[k + 1, B:, own] = jnp.concatenate([a1s[1], a2s[1]], 1)
        w21 = split(-prod(w2s, split(low1), NN))
        for part in range(2):
            first = part * B
            w_low[k, first : first + H, :H] = w1s[part]
            w_low[k, first : first + H, H:] = jnp.zeros((H, H), bf16)
            w_low[k, first + H : first + B, :H] = w21[part]
            w_low[k, first + H : first + B, H:] = w2s[part]

    for lo, hi, _ in CLASSES:
        zeros = jnp.zeros((2 * B, (hi - 1 - lo) * B), bf16)
        for i in range(lo, NB + 1):
            low[i, :, lo * B : (hi - 1) * B] = zeros
        y_low[:, lo * B : (hi - 1) * B] = jnp.zeros((2 * RC, (hi - 1 - lo) * B), bf16)
    panel[1] = jnp.zeros((NB + 1, B, B), f32)
    y_panel[1] = jnp.zeros((RC, B), f32)
    w_low[0] = jnp.zeros((2 * B, B), bf16)
    panel[0, NB] = jnp.zeros((B, B), f32)

    for copy in copies:
        copy.wait()
    diag[...] = gram_diag(0)
    for lo, hi, tiles in CLASSES:

        def one(k, _):
            step(k, (hi - 1) * B, tiles)
            return 0

        lax.fori_loop(lo, hi, one, 0)
    put_y(NB - 1, prod(split(y_panel[(NB - 1) % 2]), w_of(NB - 1), NT))
    for k in range(NB - 1, -1, -1):
        x = prod(split(y[:, cut(k)]), w_of(k), NN)
        o_ref[cut(k), :] = x.T.astype(bf16)
        xs = split(x)
        for j in range(k - 1, -1, -1):
            tile = low[k, :B, cut(j)], low[k, B:, cut(j)]
            y[:, cut(j)] = y[:, cut(j)] - prod(xs, tile, NN)


def factor_solve(gram, right):
    return pl.pallas_call(
        factor_kernel,
        out_shape=jax.ShapeDtypeStruct((N, RC), bf16),
        in_specs=[pl.BlockSpec(memory_space=pl.ANY), pl.BlockSpec(memory_space=pltpu.VMEM)],
        out_specs=pl.BlockSpec(memory_space=pltpu.VMEM),
        scratch_shapes=[
            pltpu.VMEM((NS, 2, 4, 4, 4, 16, 256), f32),
            pltpu.VMEM((NB + 1, 2 * B, N - B), bf16),
            pltpu.VMEM((2 * RC, N - B), bf16),
            pltpu.VMEM((RC, N), f32),
            pltpu.VMEM((NB, 2 * B, B), bf16),
            pltpu.VMEM((B, B), f32),
            pltpu.VMEM((2, NB + 1, B, B), f32),
            pltpu.VMEM((2, RC, B), f32),
            pltpu.SemaphoreType.DMA((NS,)),
        ],
        compiler_params=pltpu.CompilerParams(vmem_limit_bytes=60 * 1024 * 1024),
    )(gram, right)


def local(acts, weights):
    at, wc = gather_acts(acts[0].T, weights[0])
    part, right = products(at.reshape(N, -1), wc.reshape(N, RC))
    gram, right = spread(*sum_members(part, right))
    return factor_solve(gram, right.reshape(N, RC))


def solution(mesh):
    in_specs = (P("member", None, "tp"), P("member", "tp", None))
    return jax.shard_map(
        local, mesh=mesh, in_specs=in_specs, out_specs=P(None, "tp"), check_vma=False
    )
```

```python
import jax
import jax.numpy as jnp
from jax import lax
from jax.experimental import pallas as pl
from jax.experimental.pallas import tpu as pltpu
from jax.sharding import PartitionSpec as P

f32, bf16 = jnp.float32, jnp.bfloat16
SHRINK = 0.9
B = 256
H = 128
NT = (((1,), (1,)), ((), ()))
NN = (((1,), (0,)), ((), ()))


def split(x):
    hi = x.astype(bf16)
    return hi, (x - hi.astype(f32)).astype(bf16)


def mm(a, b, dims=NN):
    return lax.dot_general(a, b, dims, preferred_element_type=f32)


def mm3(a, b, dims=NN):
    ah, al = split(a)
    bh, bl = split(b)
    return mm(ah, bh, dims) + (mm(ah, bl, dims) + mm(al, bh, dims))


def tree_sum(terms):
    while len(terms) > 1:
        pairs = [terms[i] + terms[i + 1] for i in range(0, len(terms) - 1, 2)]
        terms = pairs + terms[len(pairs) * 2 :]
    return terms[0]


def inverse_factor(block):
    groups = H // 8
    lane = lax.broadcasted_iota(jnp.int32, (8, H), 1)
    sub = lax.broadcasted_iota(jnp.int32, (8, H), 0)
    a = [block[8 * g : 8 * g + 8, :] for g in range(groups)]
    out = []
    for t in range(groups):
        base = 8 * t
        slab = a[t]
        in_block = (lane >= base) & (lane < base + 8)
        rows = [jnp.broadcast_to(slab[i : i + 1, :], (8, H)) for i in range(8)]
        e = [
            [jnp.broadcast_to(rows[i][:, base + c : base + c + 1], (8, H)) for c in range(i + 1)]
            for i in range(8)
        ]
        r = [jnp.where(in_block, (lane == base + i).astype(f32), rows[i]) for i in range(8)]
        inv = [None] * 8
        piv = [None] * 8
        low = [[None] * 8 for _ in range(8)]
        unit = [[None] * 8 for _ in range(8)]

        def eliminate(c, i):
            r[i] = r[i] - low[i][c] * r[c]
            for j in range(c):
                unit[i][j] = unit[i][j] - low[i][c] * unit[c][j]
            unit[i][c] = -low[i][c]

        for c in range(0, 8, 2):
            d = c + 1
            p, q, s = e[c][c], e[d][c], e[d][d]
            det = p * s - q * q
            inv_p = pl.reciprocal(p, approx=True)
            inv_det = pl.reciprocal(det, approx=True)
            inv[c], inv[d] = inv_p, p * inv_det
            piv[c], piv[d] = p, det * inv_p
            low[d][c] = q * inv_p
            left = {i: e[i][c] * s - e[i][d] * q for i in range(c + 2, 8)}
            right = {i: e[i][d] * p - e[i][c] * q for i in range(c + 2, 8)}
            for i in range(c + 2, 8):
                for j in range(c + 2, i + 1):
                    e[i][j] = e[i][j] - (left[i] * e[j][c] + right[i] * e[j][d]) * inv_det
                low[i][c] = e[i][c] * inv_p
                low[i][d] = right[i] * inv_det
            eliminate(c, d)
            for i in range(c + 2, 8):
                eliminate(c, i)
                eliminate(d, i)
        own = jnp.zeros((8, H), f32)
        for i in range(8):
            own = jnp.where(sub == i, r[i] * lax.rsqrt(piv[i]), own)
        out.append(jnp.where(lane < base + 8, own, 0.0))
        if t + 1 < groups:
            v = [r[i] * inv[i] for i in range(8)]
            z = [tree_sum([v[j]] + [unit[i][j] * v[i] for i in range(j + 1, 8)]) for j in range(8)]
            for g in range(t + 1, groups):
                old = a[g]
                column = [jnp.broadcast_to(old[:, base + j : base + j + 1], (8, H)) for j in range(8)]
                a[g] = jnp.where(in_block, 0.0, old) - tree_sum([column[j] * z[j] for j in range(8)])
    return jnp.concatenate(out, 0)

MESH = pl.DeviceIdType.MESH
TN = (((0,), (0,)), ((), ()))
NS = 7
PARTS = ((0, 3), (3, 2), (5, 2))


def place():
    m = lax.axis_index("member")
    t = lax.axis_index("tp")
    x = (t // 4) * 2 + (m // 2) % 2
    return x, m // 4, t % 4, m % 2


def device(x, y, z, c):
    return ((y * 2 + x % 2) * 2 + c, (x // 2) * 4 + z)


def greet(peers):
    barrier = pltpu.get_barrier_semaphore()
    for peer in peers:
        pl.semaphore_signal(barrier, inc=1, device_id=peer, device_id_type=MESH)
    pl.semaphore_wait(barrier, len(peers))


def remote(src, dst, send, recv, peer):
    return pltpu.make_async_remote_copy(
        src_ref=src, dst_ref=dst, send_sem=send, recv_sem=recv, device_id=peer, device_id_type=MESH
    )


def gather_kernel(a_ref, w_ref, at_ref, wc_ref, wx, send, recv, own):
    x, y, z, c = place()
    xh = x // 2
    t = xh * 4 + z
    other = (1 - xh) * 4 + z
    half = a_ref.shape[0] // 2
    partner = device((x + 2) % 4, y, z, c)
    ring = [device(x, y, (z + d) % 4, c) for d in range(4)]
    greet([partner] + ring[1:])

    def copy(i, src, dst, peer):
        made = remote(src, dst, send.at[i], recv.at[i], peer)
        made.start()
        return made

    def cols(first):
        return pl.ds(pl.multiple_of(first * 128, 128), 128)

    copies = {}
    copies[0] = copy(0, a_ref, at_ref.at[t], partner)
    copies[1] = copy(1, a_ref, at_ref.at[t], ring[1])
    copies[2] = copy(2, a_ref, at_ref.at[t], ring[3])
    far = pl.ds(pl.multiple_of((1 - xh) * 512, 512), 512)
    copies[9] = copy(9, w_ref.at[:, far], wx, partner)
    for d in range(1, 4):
        src = w_ref.at[:, cols(xh * 4 + (z + d) % 4)]
        copies[9 + d] = copy(9 + d, src, wc_ref.at[t], ring[d])
    keep_a = pltpu.make_async_copy(a_ref, at_ref.at[t], own.at[0])
    keep_a.start()
    keep_w = pltpu.make_async_copy(w_ref.at[:, cols(t)], wc_ref.at[t], own.at[1])
    keep_w.start()
    copies[0].wait_recv()
    copies[3] = copy(3, at_ref.at[other], at_ref.at[other], ring[1])
    copies[4] = copy(4, at_ref.at[other], at_ref.at[other], ring[3])
    for at, side in ((0, xh), (2, 1 - xh)):
        before = side * 4 + (z + 3) % 4
        after = side * 4 + (z + 1) % 4
        copies[1 + at].wait_recv()
        part = at_ref.at[before, pl.ds(0, half)]
        copies[5 + at] = copy(5 + at, part, part, ring[1])
        copies[2 + at].wait_recv()
        part = at_ref.at[after, pl.ds(half, half)]
        copies[6 + at] = copy(6 + at, part, part, ring[3])
    copies[9].wait_recv()
    keep_x = pltpu.make_async_copy(wx.at[:, cols(z)], wc_ref.at[other], own.at[2])
    keep_x.start()
    for d in range(1, 4):
        src = wx.at[:, cols((z + d) % 4)]
        copies[12 + d] = copy(12 + d, src, wc_ref.at[other], ring[d])
    for i in (5, 6, 7, 8, 10, 11, 12, 13, 14, 15):
        copies[i].wait_recv()
    for i in range(16):
        copies[i].wait_send()
    keep_a.wait()
    keep_w.wait()
    keep_x.wait()


def gather_acts(acts_t, weight):
    width, rows = acts_t.shape
    vmem = pl.BlockSpec(memory_space=pltpu.VMEM)
    return pl.pallas_call(
        gather_kernel,
        out_shape=(
            jax.ShapeDtypeStruct((8, width, rows), bf16),
            jax.ShapeDtypeStruct((8, width, 128), bf16),
        ),
        in_specs=[vmem, vmem],
        out_specs=(vmem, vmem),
        scratch_shapes=[
            pltpu.VMEM((width, 512), bf16),
            pltpu.SemaphoreType.DMA((16,)),
            pltpu.SemaphoreType.DMA((16,)),
            pltpu.SemaphoreType.DMA((3,)),
        ],
        compiler_params=pltpu.CompilerParams(
            collective_id=0, has_side_effects=True, vmem_limit_bytes=32 * 1024 * 1024
        ),
    )(acts_t, weight)


def product_kernel(at_ref, wc_ref, part_ref, right_ref):
    t = lax.axis_index("tp")
    projected = mm(at_ref[...], wc_ref[...], TN).astype(bf16)
    for i in range(10):
        rows = pl.ds(i * 256, 256)
        own = at_ref[rows, :]
        wide = own.astype(f32)
        diag = jnp.sum(wide * wide, axis=1, keepdims=True)
        scaled = diag * wc_ref[rows, :].astype(f32)
        right_ref[rows, :] = SHRINK * mm(own, projected) + (1.0 - SHRINK) * scaled
    for s in range(NS):
        b = jnp.minimum(s * 8 + t, 54)
        k = 0
        for j in range(1, 10):
            k = k + (b >= 10 * j - j * (j - 1) // 2).astype(jnp.int32)
        i = b - (10 * k - k * (k - 1) // 2) + k
        left = at_ref[pl.ds(pl.multiple_of(i * 256, 256), 256), :]
        right = at_ref[pl.ds(pl.multiple_of(k * 256, 256), 256), :]
        part_ref[s] = mm(left, right, NT)


def products(at, wc):
    vmem = pl.BlockSpec(memory_space=pltpu.VMEM)
    return pl.pallas_call(
        product_kernel,
        out_shape=(
            jax.ShapeDtypeStruct((NS, 256, 256), f32),
            jax.ShapeDtypeStruct((2560, 128), f32),
        ),
        in_specs=[vmem, vmem],
        out_specs=(vmem, vmem),
        compiler_params=pltpu.CompilerParams(vmem_limit_bytes=40 * 1024 * 1024),
    )(at, wc)


def sum_spread_kernel(
    g_ref, r_ref, go_ref, ro_ref, g_pair, r_pair, g_in, r_in, g_own, r_own,
    send, recv, gsend, grecv, rsend, rrecv, own,
):
    x, y, z, c = place()
    coord = (x, y, z)
    q = (x % 2) * 4 + y
    pair = device(x, y, z, 1 - c)
    peers = []
    for d in range(1, 8):
        p = (q + d) % 8
        peers.append((p, device((x // 2) * 2 + p // 4, p % 4, z, c)))

    def along(axis, shift):
        moved = list(coord)
        moved[axis] = (moved[axis] + shift) % 4
        return device(*moved, c)

    ring = [[along(axis, shift) for shift in range(4)] for axis in range(3)]
    near = [ring[axis][shift] for axis in range(3) for shift in (1, 2, 3)]
    greet([pair] + [peer for _, peer in peers] + near)

    first = [
        remote(g_ref.at[:, 1 - c], g_pair, send.at[0], recv.at[0], pair),
        remote(r_ref.at[1 - c], r_pair, send.at[1], recv.at[1], pair),
    ]
    for copy in first:
        copy.start()
    for copy in first:
        copy.wait_recv()
    g_pair[...] = g_pair[...] + g_ref[:, c]
    r_pair[...] = r_pair[...] + r_ref[c]
    second = []
    for d, (p, peer) in enumerate(peers):
        second.append(remote(g_pair.at[:, p], g_in.at[d], send.at[2 + d], recv.at[2 + d], peer))
        second.append(remote(r_pair.at[p], r_in.at[d], send.at[9 + d], recv.at[9 + d], peer))
    for copy in second:
        copy.start()
    for copy in second:
        copy.wait_recv()
    g_sum = g_pair[:, q]
    r_sum = r_pair[q]
    for d in range(7):
        g_sum = g_sum + g_in[d]
        r_sum = r_sum + r_in[d]
    g_own[...] = g_sum
    r_own[...] = r_sum
    started = first + second

    keep_g = pltpu.make_async_copy(g_own, go_ref.at[:, c, x, y, z], own.at[0])
    keep_r = pltpu.make_async_copy(r_own, ro_ref.at[c * 8 + q], own.at[1])
    keep_g.start()
    keep_r.start()

    def view(p, phase, value, rows=None):
        order = (p, (p + 1) % 3, (p + 2) % 3)
        index = list(coord)
        for axis in order[:phase]:
            index[axis] = pl.ds(0, 4)
        index[order[phase]] = value
        start, count = PARTS[p]
        index = [pl.ds(start, count), c] + index
        if rows is not None:
            index.append(pl.ds(rows, 8))
        return go_ref.at[tuple(index)]

    def copy(ref, sems, i, peer, src=None):
        made = remote(ref if src is None else src, ref, sems[0].at[i], sems[1].at[i], peer)
        made.start()
        started.append(made)
        return made

    g_sems, r_sems = (gsend, grecv), (rsend, rrecv)
    for phase in range(2):
        waits = []
        for p in range(3):
            axis = (p + phase) % 3
            mine = view(p, phase, coord[axis])
            base = (p * 3 + phase) * 4
            source = g_own.at[pl.ds(*PARTS[p])] if phase == 0 else None
            for n, shift in enumerate((2, 1, 3)):
                waits.append(copy(mine, g_sems, base + n, ring[axis][shift], source))
        if phase == 0:
            r_copies = [
                copy(ro_ref.at[c * 8 + q], r_sems, d, peer, r_own)
                for d, (_, peer) in enumerate(peers)
            ]
            keep_g.wait()
            keep_r.wait()
        for made in waits:
            made.wait_recv()
    last = []
    hops = []
    for p in range(3):
        axis = (p + 2) % 3
        mine = view(p, 2, coord[axis])
        base = (p * 3 + 2) * 4
        hops.append((copy(mine, g_sems, base, ring[axis][1]), copy(mine, g_sems, base + 1, ring[axis][3])))
        last.append(copy(mine, g_sems, 36 + p * 4, pair))
    for made in r_copies:
        made.wait_recv()
    last.append(copy(ro_ref.at[pl.ds(pl.multiple_of(c * 8, 8), 8)], r_sems, 7, pair))
    forwards = []
    for p in range(3):
        axis = (p + 2) % 3
        base = (p * 3 + 2) * 4
        before, after = (coord[axis] + 3) % 4, (coord[axis] + 1) % 4
        hops[p][0].wait_recv()
        one = copy(view(p, 2, before, 0), g_sems, base + 2, ring[axis][1])
        hops[p][1].wait_recv()
        two = copy(view(p, 2, after, 8), g_sems, base + 3, ring[axis][3])
        forwards.append((one, two))
        last.append(copy(view(p, 2, before), g_sems, 37 + p * 4, pair))
        last.append(copy(view(p, 2, after), g_sems, 38 + p * 4, pair))
    for p in range(3):
        axis = (p + 2) % 3
        for made in forwards[p]:
            made.wait_recv()
        far = (coord[axis] + 2) % 4
        last.append(copy(view(p, 2, far), g_sems, 39 + p * 4, pair))
    for made in last:
        made.wait_recv()
    for made in started:
        made.wait_send()


def sum_spread(part, right):
    hbm = pl.BlockSpec(memory_space=pl.ANY)
    vmem = pl.BlockSpec(memory_space=pltpu.VMEM)
    return pl.pallas_call(
        sum_spread_kernel,
        out_shape=(
            jax.ShapeDtypeStruct((NS, 2, 4, 4, 4, 16, 256), f32),
            jax.ShapeDtypeStruct((16, 160, 128), f32),
        ),
        in_specs=[vmem, vmem],
        out_specs=(hbm, hbm),
        scratch_shapes=[
            pltpu.VMEM((NS, 8, 16, 256), f32),
            pltpu.VMEM((8, 160, 128), f32),
            pltpu.VMEM((7, NS, 16, 256), f32),
            pltpu.VMEM((7, 160, 128), f32),
            pltpu.VMEM((NS, 16, 256), f32),
            pltpu.VMEM((160, 128), f32),
            pltpu.SemaphoreType.DMA((16,)),
            pltpu.SemaphoreType.DMA((16,)),
            pltpu.SemaphoreType.DMA((48,)),
            pltpu.SemaphoreType.DMA((48,)),
            pltpu.SemaphoreType.DMA((8,)),
            pltpu.SemaphoreType.DMA((8,)),
            pltpu.SemaphoreType.DMA((2,)),
        ],
        compiler_params=pltpu.CompilerParams(
            collective_id=3, has_side_effects=True, vmem_limit_bytes=40 * 1024 * 1024
        ),
    )(part.reshape(NS, 2, 8, 16, 256), right.reshape(2, 8, 160, 128))

N = 2560
NB = N // B
RC = 128
CLASSES = ((0, 3, 9), (3, 6, 6), (6, 10, 3))


def cut(k, width=B):
    return slice(k * B, k * B + width)


def prod(left, right, dims):
    lh, ll = left
    rh, rl = right
    return mm(lh, rh, dims) + (mm(ll, rh, dims) + mm(lh, rl, dims))


def chain(left, right, dims):
    lh, ll = left
    rh, rl = right
    axis = dims[0][1][0]
    return mm(jnp.concatenate([lh, ll, lh], 1), jnp.concatenate([rh, rh, rl], axis), dims)


def factor_kernel(
    g_hbm, r_ref, o_ref, g, low, y_low, y, w_low, diag, panel, y_panel,
    second, rest, l21_low, a1_low, low1_low, live, sems,
):
    row = lax.broadcasted_iota(jnp.int32, (B, B), 0)
    col = lax.broadcasted_iota(jnp.int32, (B, B), 1)

    copies = [pltpu.make_async_copy(g_hbm.at[s], g.at[s], sems.at[s]) for s in range(NS)]
    for copy in copies:
        copy.start()

    live[0] = 1

    def lanes(k):
        return pl.ds(pl.multiple_of(k * B, B), B)

    def gram(i, k):
        b = jnp.minimum(10 * k - k * (k - 1) // 2 + i - k, 54)
        s, t = b // 8, b % 8
        tile = g[s, :, pl.ds((t // 4) * 2, 2), :, t % 4].reshape(B, B)
        return tile

    def gram_diag(k):
        tile = gram(k, k)
        return jnp.where(row == col, tile, SHRINK * tile)

    def rows_of(i, width):
        return low[i, :B, :width], low[i, B:, :width]

    def put(i, k, value):
        h, l = split(value)
        low[i, :B, lanes(k)] = h
        low[i, B:, lanes(k)] = l

    def put_y(k, value):
        y[:, lanes(k)] = value
        if isinstance(k, int) and k == NB - 1:
            return
        h, l = split(value)
        y_low[:RC, lanes(k)] = h
        y_low[RC:, lanes(k)] = l

    def w_of(k):
        return w_low[k, :B, :], w_low[k, B:, :]

    def step(k, width, tiles):
        if width == CLASSES[0][1] * B - B:

            @pl.when(k == 1)
            def _():
                for copy in copies[2:]:
                    copy.wait()

        old, now = (k + 1) % 2, k % 2
        last = jnp.maximum(k - 1, 0)
        targets = [jnp.minimum(k + 1 + r, NB) for r in range(tiles)]
        early = tiles // 3 + 1
        here = rows_of(k, width)

        def update(i):
            panel[now, i] = SHRINK * gram(i, k) - prod(rows_of(i, width), here, NT)

        @pl.when(live[0] == 1)
        def _():
            w1 = split(inverse_factor(diag[:H, :H]))
            w_old = w_of(last)
            for i in targets:
                put(i, last, prod(split(panel[old, i]), w_old, NT))
            put_y(last, prod(split(y_panel[old]), w_old, NT))
            for i in targets[:early]:
                update(i)
            for part in range(2):
                first = part * B
                w_low[k, first : first + H, :H] = w1[part]
                w_low[k, first : first + H, H:] = jnp.zeros((H, H), bf16)

        def w1_of():
            return w_low[k, :H, :H], w_low[k, B : B + H, :H]

        @pl.when(live[0] == 1)
        def _():
            l21 = chain(split(diag[H:, :H]), w1_of(), NT)
            l21s = split(l21)
            l21_low[...] = l21
            second[...] = diag[H:, H:] - chain(l21s, l21s, NT)

        @pl.when(live[0] == 1)
        def _():
            w2 = split(inverse_factor(second[...]))
            for i in targets[early:]:
                update(i)
            y_rows = y_low[:RC, :width], y_low[RC:, :width]
            y_panel[now] = r_ref[lanes(k), :].T - prod(y_rows, here, NT)
            mine = rows_of(k + 1, width)
            after = gram_diag(k + 1) - prod(mine, mine, NT)
            value = panel[now, k + 1]
            a1 = chain(split(value[:, :H]), w1_of(), NT)
            a1s = split(a1)
            a1_low[...] = a1
            diag[...] = after - chain(a1s, a1s, NT)
            rest[...] = value[:, H:] - chain(a1s, split(l21_low[...]), NT)
            low1_low[...] = chain(split(l21_low[...]), w1_of(), NN)
            for part in range(2):
                first = part * B + H
                w_low[k, first : first + H, H:] = w2[part]

        @pl.when(live[0] == 1)
        def _():
            w2s = w_low[k, H:B, H:], w_low[k, B + H :, H:]
            a2s = split(chain(split(rest[...]), w2s, NT))
            diag[...] = diag[...] - chain(a2s, a2s, NT)
            own = lanes(jnp.minimum(k, NB - 2))
            a1s = split(a1_low[...])
            low[k + 1, :B, own] = jnp.concatenate([a1s[0], a2s[0]], 1)
            low[k + 1, B:, own] = jnp.concatenate([a1s[1], a2s[1]], 1)
            w21 = split(-chain(w2s, split(low1_low[...]), NN))
            for part in range(2):
                first = part * B + H
                w_low[k, first : first + H, :H] = w21[part]

    for lo, hi, _ in CLASSES:
        zeros = jnp.zeros((2 * B, (hi - 1 - lo) * B), bf16)
        for i in range(lo, NB + 1):
            low[i, :, lo * B : (hi - 1) * B] = zeros
        y_low[:, lo * B : (hi - 1) * B] = jnp.zeros((2 * RC, (hi - 1 - lo) * B), bf16)
    panel[1] = jnp.zeros((NB + 1, B, B), f32)
    y_panel[1] = jnp.zeros((RC, B), f32)
    w_low[0] = jnp.zeros((2 * B, B), bf16)
    panel[0, NB] = jnp.zeros((B, B), f32)

    for copy in copies[:2]:
        copy.wait()
    diag[...] = gram_diag(0)
    for lo, hi, tiles in CLASSES:

        def one(k, _):
            step(k, (hi - 1) * B, tiles)
            return 0

        lax.fori_loop(lo, hi, one, 0)
    put_y(NB - 1, prod(split(y_panel[(NB - 1) % 2]), w_of(NB - 1), NT))
    for k in range(NB - 1, -1, -1):
        x = prod(split(y[:, cut(k)]), w_of(k), NN)
        o_ref[cut(k), :] = x.T.astype(bf16)
        xs = split(x)
        for j in range(k - 1, -1, -1):
            tile = low[k, :B, cut(j)], low[k, B:, cut(j)]
            y[:, cut(j)] = y[:, cut(j)] - prod(xs, tile, NN)


def factor_solve(gram, right):
    return pl.pallas_call(
        factor_kernel,
        out_shape=jax.ShapeDtypeStruct((N, RC), bf16),
        in_specs=[pl.BlockSpec(memory_space=pl.ANY), pl.BlockSpec(memory_space=pltpu.VMEM)],
        out_specs=pl.BlockSpec(memory_space=pltpu.VMEM),
        scratch_shapes=[
            pltpu.VMEM((NS, 2, 4, 4, 4, 16, 256), f32),
            pltpu.VMEM((NB + 1, 2 * B, N - B), bf16),
            pltpu.VMEM((2 * RC, N - B), bf16),
            pltpu.VMEM((RC, N), f32),
            pltpu.VMEM((NB, 2 * B, B), bf16),
            pltpu.VMEM((B, B), f32),
            pltpu.VMEM((2, NB + 1, B, B), f32),
            pltpu.VMEM((2, RC, B), f32),
            pltpu.VMEM((H, H), f32),
            pltpu.VMEM((B, H), f32),
            pltpu.VMEM((H, H), f32),
            pltpu.VMEM((B, H), f32),
            pltpu.VMEM((H, H), f32),
            pltpu.SMEM((1,), jnp.int32),
            pltpu.SemaphoreType.DMA((NS,)),
        ],
        compiler_params=pltpu.CompilerParams(vmem_limit_bytes=60 * 1024 * 1024),
    )(gram, right)


def local(acts, weights):
    at, wc = gather_acts(acts[0].T, weights[0])
    part, right = products(at.reshape(N, -1), wc.reshape(N, RC))
    gram, right = sum_spread(part, right)
    return factor_solve(gram, right.reshape(N, RC))


def solution(mesh):
    in_specs = (P("member", None, "tp"), P("member", "tp", None))
    return jax.shard_map(
        local, mesh=mesh, in_specs=in_specs, out_specs=P(None, "tp"), check_vma=False
    )
```

```python
import jax
import jax.numpy as jnp
from jax import lax
from jax.experimental import pallas as pl
from jax.experimental.pallas import tpu as pltpu
from jax.sharding import PartitionSpec as P

f32, bf16 = jnp.float32, jnp.bfloat16
SHRINK = 0.9
B = 256
H = 128
NT = (((1,), (1,)), ((), ()))
NN = (((1,), (0,)), ((), ()))


def split(x):
    hi = x.astype(bf16)
    return hi, (x - hi.astype(f32)).astype(bf16)


def mm(a, b, dims=NN):
    return lax.dot_general(a, b, dims, preferred_element_type=f32)


def mm3(a, b, dims=NN):
    ah, al = split(a)
    bh, bl = split(b)
    return mm(ah, bh, dims) + (mm(ah, bl, dims) + mm(al, bh, dims))


def tree_sum(terms):
    while len(terms) > 1:
        pairs = [terms[i] + terms[i + 1] for i in range(0, len(terms) - 1, 2)]
        terms = pairs + terms[len(pairs) * 2 :]
    return terms[0]


def inverse_factor(block):
    groups = H // 8
    lane = lax.broadcasted_iota(jnp.int32, (8, H), 1)
    sub = lax.broadcasted_iota(jnp.int32, (8, H), 0)
    a = [block[8 * g : 8 * g + 8, :] for g in range(groups)]
    out = []
    for t in range(groups):
        base = 8 * t
        slab = a[t]
        in_block = (lane >= base) & (lane < base + 8)
        rows = [jnp.broadcast_to(slab[i : i + 1, :], (8, H)) for i in range(8)]
        e = [
            [jnp.broadcast_to(rows[i][:, base + c : base + c + 1], (8, H)) for c in range(i + 1)]
            for i in range(8)
        ]
        r = [jnp.where(in_block, (lane == base + i).astype(f32), rows[i]) for i in range(8)]
        inv = [None] * 8
        piv = [None] * 8
        low = [[None] * 8 for _ in range(8)]
        unit = [[None] * 8 for _ in range(8)]

        def eliminate(c, i):
            r[i] = r[i] - low[i][c] * r[c]
            for j in range(c):
                unit[i][j] = unit[i][j] - low[i][c] * unit[c][j]
            unit[i][c] = -low[i][c]

        for c in range(0, 8, 2):
            d = c + 1
            p, q, s = e[c][c], e[d][c], e[d][d]
            det = p * s - q * q
            inv_p = pl.reciprocal(p, approx=True)
            inv_det = pl.reciprocal(det, approx=True)
            inv[c], inv[d] = inv_p, p * inv_det
            piv[c], piv[d] = p, det * inv_p
            low[d][c] = q * inv_p
            left = {i: e[i][c] * s - e[i][d] * q for i in range(c + 2, 8)}
            right = {i: e[i][d] * p - e[i][c] * q for i in range(c + 2, 8)}
            for i in range(c + 2, 8):
                for j in range(c + 2, i + 1):
                    e[i][j] = e[i][j] - (left[i] * e[j][c] + right[i] * e[j][d]) * inv_det
                low[i][c] = e[i][c] * inv_p
                low[i][d] = right[i] * inv_det
            eliminate(c, d)
            for i in range(c + 2, 8):
                eliminate(c, i)
                eliminate(d, i)
        own = jnp.zeros((8, H), f32)
        for i in range(8):
            own = jnp.where(sub == i, r[i] * lax.rsqrt(piv[i]), own)
        out.append(jnp.where(lane < base + 8, own, 0.0))
        if t + 1 < groups:
            v = [r[i] * inv[i] for i in range(8)]
            z = [tree_sum([v[j]] + [unit[i][j] * v[i] for i in range(j + 1, 8)]) for j in range(8)]
            for g in range(t + 1, groups):
                old = a[g]
                column = [jnp.broadcast_to(old[:, base + j : base + j + 1], (8, H)) for j in range(8)]
                a[g] = jnp.where(in_block, 0.0, old) - tree_sum([column[j] * z[j] for j in range(8)])
    return jnp.concatenate(out, 0)

MESH = pl.DeviceIdType.MESH
TN = (((0,), (0,)), ((), ()))
NS = 7
PARTS = ((0, 0, 2, None), (1, 2, 2, None), (2, 4, 2, None), (0, 6, 1, 0), (1, 6, 1, 8))


def place():
    m = lax.axis_index("member")
    t = lax.axis_index("tp")
    x = (t // 4) * 2 + (m // 2) % 2
    return x, m // 4, t % 4, m % 2


def device(x, y, z, c):
    return ((y * 2 + x % 2) * 2 + c, (x // 2) * 4 + z)


def greet(peers):
    barrier = pltpu.get_barrier_semaphore()
    for peer in peers:
        pl.semaphore_signal(barrier, inc=1, device_id=peer, device_id_type=MESH)
    pl.semaphore_wait(barrier, len(peers))


def remote(src, dst, send, recv, peer):
    return pltpu.make_async_remote_copy(
        src_ref=src, dst_ref=dst, send_sem=send, recv_sem=recv, device_id=peer, device_id_type=MESH
    )


def gather_kernel(a_ref, w_ref, at_ref, wc_ref, wx, send, recv, own):
    x, y, z, c = place()
    xh = x // 2
    t = xh * 4 + z
    other = (1 - xh) * 4 + z
    half = a_ref.shape[0] // 2
    partner = device((x + 2) % 4, y, z, c)
    ring = [device(x, y, (z + d) % 4, c) for d in range(4)]
    greet([partner] + ring[1:])

    def copy(i, src, dst, peer):
        made = remote(src, dst, send.at[i], recv.at[i], peer)
        made.start()
        return made

    def cols(first):
        return pl.ds(pl.multiple_of(first * 128, 128), 128)

    copies = {}
    copies[0] = copy(0, a_ref, at_ref.at[t], partner)
    copies[1] = copy(1, a_ref, at_ref.at[t], ring[1])
    copies[2] = copy(2, a_ref, at_ref.at[t], ring[3])
    far = pl.ds(pl.multiple_of((1 - xh) * 512, 512), 512)
    copies[9] = copy(9, w_ref.at[:, far], wx, partner)
    for d in range(1, 4):
        src = w_ref.at[:, cols(xh * 4 + (z + d) % 4)]
        copies[9 + d] = copy(9 + d, src, wc_ref.at[t], ring[d])
    keep_a = pltpu.make_async_copy(a_ref, at_ref.at[t], own.at[0])
    keep_a.start()
    keep_w = pltpu.make_async_copy(w_ref.at[:, cols(t)], wc_ref.at[t], own.at[1])
    keep_w.start()
    copies[0].wait_recv()
    copies[3] = copy(3, at_ref.at[other], at_ref.at[other], ring[1])
    copies[4] = copy(4, at_ref.at[other], at_ref.at[other], ring[3])
    for at, side in ((0, xh), (2, 1 - xh)):
        before = side * 4 + (z + 3) % 4
        after = side * 4 + (z + 1) % 4
        copies[1 + at].wait_recv()
        part = at_ref.at[before, pl.ds(0, half)]
        copies[5 + at] = copy(5 + at, part, part, ring[1])
        copies[2 + at].wait_recv()
        part = at_ref.at[after, pl.ds(half, half)]
        copies[6 + at] = copy(6 + at, part, part, ring[3])
    copies[9].wait_recv()
    keep_x = pltpu.make_async_copy(wx.at[:, cols(z)], wc_ref.at[other], own.at[2])
    keep_x.start()
    for d in range(1, 4):
        src = wx.at[:, cols((z + d) % 4)]
        copies[12 + d] = copy(12 + d, src, wc_ref.at[other], ring[d])
    for i in (5, 6, 7, 8, 10, 11, 12, 13, 14, 15):
        copies[i].wait_recv()
    for i in range(16):
        copies[i].wait_send()
    keep_a.wait()
    keep_w.wait()
    keep_x.wait()


def gather_acts(acts_t, weight):
    width, rows = acts_t.shape
    vmem = pl.BlockSpec(memory_space=pltpu.VMEM)
    return pl.pallas_call(
        gather_kernel,
        out_shape=(
            jax.ShapeDtypeStruct((8, width, rows), bf16),
            jax.ShapeDtypeStruct((8, width, 128), bf16),
        ),
        in_specs=[vmem, vmem],
        out_specs=(vmem, vmem),
        scratch_shapes=[
            pltpu.VMEM((width, 512), bf16),
            pltpu.SemaphoreType.DMA((16,)),
            pltpu.SemaphoreType.DMA((16,)),
            pltpu.SemaphoreType.DMA((3,)),
        ],
        compiler_params=pltpu.CompilerParams(
            collective_id=0, has_side_effects=True, vmem_limit_bytes=32 * 1024 * 1024
        ),
    )(acts_t, weight)


def product_kernel(at_ref, wc_ref, part_ref, right_ref):
    t = lax.axis_index("tp")
    projected = mm(at_ref[...], wc_ref[...], TN).astype(bf16)
    for i in range(10):
        rows = pl.ds(i * 256, 256)
        own = at_ref[rows, :]
        wide = own.astype(f32)
        diag = jnp.sum(wide * wide, axis=1, keepdims=True)
        scaled = diag * wc_ref[rows, :].astype(f32)
        right_ref[rows, :] = SHRINK * mm(own, projected) + (1.0 - SHRINK) * scaled
    for s in range(NS):
        b = jnp.minimum(s * 8 + t, 54)
        k = 0
        for j in range(1, 10):
            k = k + (b >= 10 * j - j * (j - 1) // 2).astype(jnp.int32)
        i = b - (10 * k - k * (k - 1) // 2) + k
        left = at_ref[pl.ds(pl.multiple_of(i * 256, 256), 256), :]
        right = at_ref[pl.ds(pl.multiple_of(k * 256, 256), 256), :]
        part_ref[s] = mm(left, right, NT)


def products(at, wc):
    vmem = pl.BlockSpec(memory_space=pltpu.VMEM)
    return pl.pallas_call(
        product_kernel,
        out_shape=(
            jax.ShapeDtypeStruct((NS, 256, 256), f32),
            jax.ShapeDtypeStruct((2560, 128), f32),
        ),
        in_specs=[vmem, vmem],
        out_specs=(vmem, vmem),
        compiler_params=pltpu.CompilerParams(vmem_limit_bytes=40 * 1024 * 1024),
    )(at, wc)


def sum_spread_kernel(
    g_ref, r_ref, go_ref, ro_ref, g_pair, r_pair, g_in, r_in, g_own, r_own,
    send, recv, gsend, grecv, rsend, rrecv, own,
):
    x, y, z, c = place()
    coord = (x, y, z)
    q = (x % 2) * 4 + y
    pair = device(x, y, z, 1 - c)
    peers = []
    for d in range(1, 8):
        p = (q + d) % 8
        peers.append((p, device((x // 2) * 2 + p // 4, p % 4, z, c)))

    def along(axis, shift):
        moved = list(coord)
        moved[axis] = (moved[axis] + shift) % 4
        return device(*moved, c)

    ring = [[along(axis, shift) for shift in range(4)] for axis in range(3)]
    near = [ring[axis][shift] for axis in range(3) for shift in (1, 2, 3)]
    greet([pair] + [peer for _, peer in peers] + near)

    first = [
        remote(g_ref.at[:, 1 - c], g_pair, send.at[0], recv.at[0], pair),
        remote(r_ref.at[1 - c], r_pair, send.at[1], recv.at[1], pair),
    ]
    for copy in first:
        copy.start()
    for copy in first:
        copy.wait_recv()
    g_pair[...] = g_pair[...] + g_ref[:, c]
    r_pair[...] = r_pair[...] + r_ref[c]
    second = []
    for d, (p, peer) in enumerate(peers):
        second.append(remote(g_pair.at[:, p], g_in.at[d], send.at[2 + d], recv.at[2 + d], peer))
        second.append(remote(r_pair.at[p], r_in.at[d], send.at[9 + d], recv.at[9 + d], peer))
    for copy in second:
        copy.start()
    for copy in second:
        copy.wait_recv()
    g_sum = g_pair[:, q]
    r_sum = r_pair[q]
    for d in range(7):
        g_sum = g_sum + g_in[d]
        r_sum = r_sum + r_in[d]
    g_own[...] = g_sum
    r_own[...] = r_sum
    started = first + second

    keep_g = pltpu.make_async_copy(g_own, go_ref.at[:, c, x, y, z], own.at[0])
    keep_r = pltpu.make_async_copy(r_own, ro_ref.at[c * 8 + q], own.at[1])
    keep_g.start()
    keep_r.start()

    def turn(n, phase):
        return (PARTS[n][0] + phase) % 3

    def view(n, phase, value, half=None):
        axis, start, count, row = PARTS[n]
        index = list(coord)
        for earlier in range(phase):
            index[(axis + earlier) % 3] = pl.ds(0, 4)
        index[(axis + phase) % 3] = value
        index = [pl.ds(start, count), c] + index
        if row is not None:
            index.append(pl.ds(row, 8))
            if half is not None:
                index.append(pl.ds(128 * half, 128))
        elif half is not None:
            index.append(pl.ds(8 * half, 8))
        return go_ref.at[tuple(index)]

    def own_part(n):
        _, start, count, row = PARTS[n]
        if row is None:
            return g_own.at[pl.ds(start, count)]
        return g_own.at[pl.ds(start, count), pl.ds(row, 8)]

    def copy(ref, sems, i, peer, src=None):
        made = remote(ref if src is None else src, ref, sems[0].at[i], sems[1].at[i], peer)
        made.start()
        started.append(made)
        return made

    g_sems, r_sems = (gsend, grecv), (rsend, rrecv)
    order = (2, 1, 4, 0, 3)

    def spread_along(p, phase):
        axis = turn(p, phase)
        mine = view(p, phase, coord[axis])
        base = p * 14 + phase * 3
        source = own_part(p) if phase == 0 else None
        return [
            copy(mine, g_sems, base + n, ring[axis][shift], source)
            for n, shift in enumerate((2, 1, 3))
        ]

    flying = {p: spread_along(p, 0) for p in range(5)}
    keep_g.wait()
    for p in order:
        for made in flying[p]:
            made.wait_recv()
        flying[p] = spread_along(p, 1)
    r_copies = [
        copy(ro_ref.at[c * 8 + q], r_sems, d, peer, r_own) for d, (_, peer) in enumerate(peers)
    ]
    last = []
    for p in order:
        for made in flying[p]:
            made.wait_recv()
        axis = turn(p, 2)
        mine = view(p, 2, coord[axis])
        base = p * 14 + 6
        flying[p] = (
            copy(mine, g_sems, base, ring[axis][1]),
            copy(mine, g_sems, base + 1, ring[axis][3]),
        )
        last.append(copy(mine, g_sems, p * 14 + 10, pair))
    for p in order:
        axis = turn(p, 2)
        base = p * 14 + 6
        before, after = (coord[axis] + 3) % 4, (coord[axis] + 1) % 4
        one, two = flying[p]
        one.wait_recv()
        three = copy(view(p, 2, before, 0), g_sems, base + 2, ring[axis][1])
        two.wait_recv()
        four = copy(view(p, 2, after, 1), g_sems, base + 3, ring[axis][3])
        flying[p] = (three, four)
        last.append(copy(view(p, 2, before), g_sems, p * 14 + 11, pair))
        last.append(copy(view(p, 2, after), g_sems, p * 14 + 12, pair))
    keep_r.wait()
    for made in r_copies:
        made.wait_recv()
    last.append(copy(ro_ref.at[pl.ds(pl.multiple_of(c * 8, 8), 8)], r_sems, 7, pair))
    for p in order:
        axis = turn(p, 2)
        for made in flying[p]:
            made.wait_recv()
        far = (coord[axis] + 2) % 4
        last.append(copy(view(p, 2, far), g_sems, p * 14 + 13, pair))
    for made in last:
        made.wait_recv()
    for made in started:
        made.wait_send()


def sum_spread(part, right):
    hbm = pl.BlockSpec(memory_space=pl.ANY)
    vmem = pl.BlockSpec(memory_space=pltpu.VMEM)
    return pl.pallas_call(
        sum_spread_kernel,
        out_shape=(
            jax.ShapeDtypeStruct((NS, 2, 4, 4, 4, 16, 256), f32),
            jax.ShapeDtypeStruct((16, 160, 128), f32),
        ),
        in_specs=[vmem, vmem],
        out_specs=(hbm, hbm),
        scratch_shapes=[
            pltpu.VMEM((NS, 8, 16, 256), f32),
            pltpu.VMEM((8, 160, 128), f32),
            pltpu.VMEM((7, NS, 16, 256), f32),
            pltpu.VMEM((7, 160, 128), f32),
            pltpu.VMEM((NS, 16, 256), f32),
            pltpu.VMEM((160, 128), f32),
            pltpu.SemaphoreType.DMA((16,)),
            pltpu.SemaphoreType.DMA((16,)),
            pltpu.SemaphoreType.DMA((70,)),
            pltpu.SemaphoreType.DMA((70,)),
            pltpu.SemaphoreType.DMA((8,)),
            pltpu.SemaphoreType.DMA((8,)),
            pltpu.SemaphoreType.DMA((2,)),
        ],
        compiler_params=pltpu.CompilerParams(
            collective_id=3, has_side_effects=True, vmem_limit_bytes=40 * 1024 * 1024
        ),
    )(part.reshape(NS, 2, 8, 16, 256), right.reshape(2, 8, 160, 128))

N = 2560
NB = N // B
RC = 128
CLASSES = ((0, 3, 9), (3, 6, 6), (6, 10, 3))


def cut(k, width=B):
    return slice(k * B, k * B + width)


def prod(left, right, dims):
    lh, ll = left
    rh, rl = right
    return mm(lh, rh, dims) + (mm(ll, rh, dims) + mm(lh, rl, dims))


def chain(left, right, dims):
    lh, ll = left
    rh, rl = right
    axis = dims[0][1][0]
    return mm(jnp.concatenate([lh, ll, lh], 1), jnp.concatenate([rh, rh, rl], axis), dims)


def factor_kernel(
    g_hbm, r_ref, o_ref, g, low, y_low, y, w_low, diag, panel, y_panel,
    second, rest, l21_low, a1_low, low1_low, live, sems,
):
    row = lax.broadcasted_iota(jnp.int32, (B, B), 0)
    col = lax.broadcasted_iota(jnp.int32, (B, B), 1)

    copies = [pltpu.make_async_copy(g_hbm.at[s], g.at[s], sems.at[s]) for s in range(NS)]
    for copy in copies:
        copy.start()

    live[0] = 1

    def lanes(k):
        return pl.ds(pl.multiple_of(k * B, B), B)

    def gram(i, k):
        b = jnp.minimum(10 * k - k * (k - 1) // 2 + i - k, 54)
        s, t = b // 8, b % 8
        tile = g[s, :, pl.ds((t // 4) * 2, 2), :, t % 4].reshape(B, B)
        return tile

    def gram_diag(k):
        tile = gram(k, k)
        return jnp.where(row == col, tile, SHRINK * tile)

    def rows_of(i, width):
        return low[i, :B, :width], low[i, B:, :width]

    def put(i, k, value):
        h, l = split(value)
        low[i, :B, lanes(k)] = h
        low[i, B:, lanes(k)] = l

    def put_y(k, value):
        y[:, lanes(k)] = value
        if isinstance(k, int) and k == NB - 1:
            return
        h, l = split(value)
        y_low[:RC, lanes(k)] = h
        y_low[RC:, lanes(k)] = l

    def w_of(k):
        return w_low[k, :B, :], w_low[k, B:, :]

    def step(k, width, tiles):
        if width == CLASSES[0][1] * B - B:

            @pl.when(k == 1)
            def _():
                for copy in copies[2:]:
                    copy.wait()

        old, now = (k + 1) % 2, k % 2
        last = jnp.maximum(k - 1, 0)
        targets = [jnp.minimum(k + 1 + r, NB) for r in range(tiles)]
        early = tiles // 3 + 1
        here = rows_of(k, width)

        def update(i):
            panel[now, i] = SHRINK * gram(i, k) - prod(rows_of(i, width), here, NT)

        @pl.when(live[0] == 1)
        def _():
            w1 = split(inverse_factor(diag[:H, :H]))
            w_old = w_of(last)
            for i in targets:
                put(i, last, prod(split(panel[old, i]), w_old, NT))
            put_y(last, prod(split(y_panel[old]), w_old, NT))
            for i in targets[:early]:
                update(i)
            for part in range(2):
                first = part * B
                w_low[k, first : first + H, :H] = w1[part]
                w_low[k, first : first + H, H:] = jnp.zeros((H, H), bf16)

        def w1_of():
            return w_low[k, :H, :H], w_low[k, B : B + H, :H]

        @pl.when(live[0] == 1)
        def _():
            l21 = chain(split(diag[H:, :H]), w1_of(), NT)
            l21s = split(l21)
            l21_low[...] = l21
            second[...] = diag[H:, H:] - chain(l21s, l21s, NT)

        @pl.when(live[0] == 1)
        def _():
            w2 = split(inverse_factor(second[...]))
            for i in targets[early:]:
                update(i)
            y_rows = y_low[:RC, :width], y_low[RC:, :width]
            y_panel[now] = r_ref[lanes(k), :].T - prod(y_rows, here, NT)
            mine = rows_of(k + 1, width)
            after = gram_diag(k + 1) - prod(mine, mine, NT)
            value = panel[now, k + 1]
            a1 = chain(split(value[:, :H]), w1_of(), NT)
            a1s = split(a1)
            a1_low[...] = a1
            diag[...] = after - chain(a1s, a1s, NT)
            rest[...] = value[:, H:] - chain(a1s, split(l21_low[...]), NT)
            low1_low[...] = chain(split(l21_low[...]), w1_of(), NN)
            for part in range(2):
                first = part * B + H
                w_low[k, first : first + H, H:] = w2[part]

        @pl.when(live[0] == 1)
        def _():
            w2s = w_low[k, H:B, H:], w_low[k, B + H :, H:]
            a2s = split(chain(split(rest[...]), w2s, NT))
            diag[...] = diag[...] - chain(a2s, a2s, NT)
            own = lanes(jnp.minimum(k, NB - 2))
            a1s = split(a1_low[...])
            low[k + 1, :B, own] = jnp.concatenate([a1s[0], a2s[0]], 1)
            low[k + 1, B:, own] = jnp.concatenate([a1s[1], a2s[1]], 1)
            w21 = split(-chain(w2s, split(low1_low[...]), NN))
            for part in range(2):
                first = part * B + H
                w_low[k, first : first + H, :H] = w21[part]

    for lo, hi, _ in CLASSES:
        zeros = jnp.zeros((2 * B, (hi - 1 - lo) * B), bf16)
        for i in range(lo, NB + 1):
            low[i, :, lo * B : (hi - 1) * B] = zeros
        y_low[:, lo * B : (hi - 1) * B] = jnp.zeros((2 * RC, (hi - 1 - lo) * B), bf16)
    panel[1] = jnp.zeros((NB + 1, B, B), f32)
    y_panel[1] = jnp.zeros((RC, B), f32)
    w_low[0] = jnp.zeros((2 * B, B), bf16)
    panel[0, NB] = jnp.zeros((B, B), f32)

    for copy in copies[:2]:
        copy.wait()
    diag[...] = gram_diag(0)
    for lo, hi, tiles in CLASSES:

        def one(k, _):
            step(k, (hi - 1) * B, tiles)
            return 0

        lax.fori_loop(lo, hi, one, 0)
    put_y(NB - 1, prod(split(y_panel[(NB - 1) % 2]), w_of(NB - 1), NT))
    for k in range(NB - 1, -1, -1):
        x = prod(split(y[:, cut(k)]), w_of(k), NN)
        o_ref[cut(k), :] = x.T.astype(bf16)
        xs = split(x)
        for j in range(k - 1, -1, -1):
            tile = low[k, :B, cut(j)], low[k, B:, cut(j)]
            y[:, cut(j)] = y[:, cut(j)] - prod(xs, tile, NN)


def factor_solve(gram, right):
    return pl.pallas_call(
        factor_kernel,
        out_shape=jax.ShapeDtypeStruct((N, RC), bf16),
        in_specs=[pl.BlockSpec(memory_space=pl.ANY), pl.BlockSpec(memory_space=pltpu.VMEM)],
        out_specs=pl.BlockSpec(memory_space=pltpu.VMEM),
        scratch_shapes=[
            pltpu.VMEM((NS, 2, 4, 4, 4, 16, 256), f32),
            pltpu.VMEM((NB + 1, 2 * B, N - B), bf16),
            pltpu.VMEM((2 * RC, N - B), bf16),
            pltpu.VMEM((RC, N), f32),
            pltpu.VMEM((NB, 2 * B, B), bf16),
            pltpu.VMEM((B, B), f32),
            pltpu.VMEM((2, NB + 1, B, B), f32),
            pltpu.VMEM((2, RC, B), f32),
            pltpu.VMEM((H, H), f32),
            pltpu.VMEM((B, H), f32),
            pltpu.VMEM((H, H), f32),
            pltpu.VMEM((B, H), f32),
            pltpu.VMEM((H, H), f32),
            pltpu.SMEM((1,), jnp.int32),
            pltpu.SemaphoreType.DMA((NS,)),
        ],
        compiler_params=pltpu.CompilerParams(vmem_limit_bytes=60 * 1024 * 1024),
    )(gram, right)


def local(acts, weights):
    at, wc = gather_acts(acts[0].T, weights[0])
    part, right = products(at.reshape(N, -1), wc.reshape(N, RC))
    gram, right = sum_spread(part, right)
    return factor_solve(gram, right.reshape(N, RC))


def solution(mesh):
    in_specs = (P("member", None, "tp"), P("member", "tp", None))
    return jax.shard_map(
        local, mesh=mesh, in_specs=in_specs, out_specs=P(None, "tp"), check_vma=False
    )
```

```python
import jax
import jax.numpy as jnp
from jax import lax
from jax.experimental import pallas as pl
from jax.experimental.pallas import tpu as pltpu
from jax.sharding import PartitionSpec as P

f32, bf16 = jnp.float32, jnp.bfloat16
SHRINK = 0.9
B = 256
H = 128
NT = (((1,), (1,)), ((), ()))
NN = (((1,), (0,)), ((), ()))


def split(x):
    hi = x.astype(bf16)
    return hi, (x - hi.astype(f32)).astype(bf16)


def mm(a, b, dims=NN):
    return lax.dot_general(a, b, dims, preferred_element_type=f32)


def mm3(a, b, dims=NN):
    ah, al = split(a)
    bh, bl = split(b)
    return mm(ah, bh, dims) + (mm(ah, bl, dims) + mm(al, bh, dims))


def tree_sum(terms):
    while len(terms) > 1:
        pairs = [terms[i] + terms[i + 1] for i in range(0, len(terms) - 1, 2)]
        terms = pairs + terms[len(pairs) * 2 :]
    return terms[0]


def inverse_factor(block):
    groups = H // 8
    lane = lax.broadcasted_iota(jnp.int32, (8, H), 1)
    sub = lax.broadcasted_iota(jnp.int32, (8, H), 0)
    a = [block[8 * g : 8 * g + 8, :] for g in range(groups)]
    out = []
    for t in range(groups):
        base = 8 * t
        slab = a[t]
        in_block = (lane >= base) & (lane < base + 8)
        rows = [jnp.broadcast_to(slab[i : i + 1, :], (8, H)) for i in range(8)]
        e = [
            [jnp.broadcast_to(rows[i][:, base + c : base + c + 1], (8, H)) for c in range(i + 1)]
            for i in range(8)
        ]
        r = [jnp.where(in_block, (lane == base + i).astype(f32), rows[i]) for i in range(8)]
        inv = [None] * 8
        piv = [None] * 8
        low = [[None] * 8 for _ in range(8)]
        unit = [[None] * 8 for _ in range(8)]

        def eliminate(c, i):
            r[i] = r[i] - low[i][c] * r[c]
            for j in range(c):
                unit[i][j] = unit[i][j] - low[i][c] * unit[c][j]
            unit[i][c] = -low[i][c]

        for c in range(0, 8, 2):
            d = c + 1
            p, q, s = e[c][c], e[d][c], e[d][d]
            det = p * s - q * q
            inv_p = pl.reciprocal(p, approx=True)
            inv_det = pl.reciprocal(det, approx=True)
            inv[c], inv[d] = inv_p, p * inv_det
            piv[c], piv[d] = p, det * inv_p
            low[d][c] = q * inv_p
            left = {i: e[i][c] * s - e[i][d] * q for i in range(c + 2, 8)}
            right = {i: e[i][d] * p - e[i][c] * q for i in range(c + 2, 8)}
            for i in range(c + 2, 8):
                for j in range(c + 2, i + 1):
                    e[i][j] = e[i][j] - (left[i] * e[j][c] + right[i] * e[j][d]) * inv_det
                low[i][c] = e[i][c] * inv_p
                low[i][d] = right[i] * inv_det
            eliminate(c, d)
            for i in range(c + 2, 8):
                eliminate(c, i)
                eliminate(d, i)
        own = jnp.zeros((8, H), f32)
        for i in range(8):
            own = jnp.where(sub == i, r[i] * lax.rsqrt(piv[i]), own)
        out.append(jnp.where(lane < base + 8, own, 0.0))
        if t + 1 < groups:
            v = [r[i] * inv[i] for i in range(8)]
            z = [tree_sum([v[j]] + [unit[i][j] * v[i] for i in range(j + 1, 8)]) for j in range(8)]
            for g in range(t + 1, groups):
                old = a[g]
                column = [jnp.broadcast_to(old[:, base + j : base + j + 1], (8, H)) for j in range(8)]
                a[g] = jnp.where(in_block, 0.0, old) - tree_sum([column[j] * z[j] for j in range(8)])
    return jnp.concatenate(out, 0)

MESH = pl.DeviceIdType.MESH
TN = (((0,), (0,)), ((), ()))
NS = 7
PARTS = ((0, 0, 2, None), (1, 2, 2, None), (2, 4, 2, None), (0, 6, 1, 0), (1, 6, 1, 8))


def place():
    m = lax.axis_index("member")
    t = lax.axis_index("tp")
    x = (t // 4) * 2 + (m // 2) % 2
    return x, m // 4, t % 4, m % 2


def device(x, y, z, c):
    return ((y * 2 + x % 2) * 2 + c, (x // 2) * 4 + z)


def greet(peers):
    barrier = pltpu.get_barrier_semaphore()
    for peer in peers:
        pl.semaphore_signal(barrier, inc=1, device_id=peer, device_id_type=MESH)
    pl.semaphore_wait(barrier, len(peers))


def remote(src, dst, send, recv, peer):
    return pltpu.make_async_remote_copy(
        src_ref=src, dst_ref=dst, send_sem=send, recv_sem=recv, device_id=peer, device_id_type=MESH
    )


def gather_kernel(a_ref, w_ref, at_ref, wc_ref, wx, send, recv, own):
    x, y, z, c = place()
    xh = x // 2
    t = xh * 4 + z
    other = (1 - xh) * 4 + z
    half = a_ref.shape[0] // 2
    partner = device((x + 2) % 4, y, z, c)
    ring = [device(x, y, (z + d) % 4, c) for d in range(4)]
    greet([partner] + ring[1:])

    def copy(i, src, dst, peer):
        made = remote(src, dst, send.at[i], recv.at[i], peer)
        made.start()
        return made

    def cols(first):
        return pl.ds(pl.multiple_of(first * 128, 128), 128)

    copies = {}
    copies[0] = copy(0, a_ref, at_ref.at[t], partner)
    copies[1] = copy(1, a_ref, at_ref.at[t], ring[1])
    copies[2] = copy(2, a_ref, at_ref.at[t], ring[3])
    far = pl.ds(pl.multiple_of((1 - xh) * 512, 512), 512)
    copies[9] = copy(9, w_ref.at[:, far], wx, partner)
    for d in range(1, 4):
        src = w_ref.at[:, cols(xh * 4 + (z + d) % 4)]
        copies[9 + d] = copy(9 + d, src, wc_ref.at[t], ring[d])
    keep_a = pltpu.make_async_copy(a_ref, at_ref.at[t], own.at[0])
    keep_a.start()
    keep_w = pltpu.make_async_copy(w_ref.at[:, cols(t)], wc_ref.at[t], own.at[1])
    keep_w.start()
    copies[0].wait_recv()
    copies[3] = copy(3, at_ref.at[other], at_ref.at[other], ring[1])
    copies[4] = copy(4, at_ref.at[other], at_ref.at[other], ring[3])
    for at, side in ((0, xh), (2, 1 - xh)):
        before = side * 4 + (z + 3) % 4
        after = side * 4 + (z + 1) % 4
        copies[1 + at].wait_recv()
        part = at_ref.at[before, pl.ds(0, half)]
        copies[5 + at] = copy(5 + at, part, part, ring[1])
        copies[2 + at].wait_recv()
        part = at_ref.at[after, pl.ds(half, half)]
        copies[6 + at] = copy(6 + at, part, part, ring[3])
    copies[9].wait_recv()
    keep_x = pltpu.make_async_copy(wx.at[:, cols(z)], wc_ref.at[other], own.at[2])
    keep_x.start()
    for d in range(1, 4):
        src = wx.at[:, cols((z + d) % 4)]
        copies[12 + d] = copy(12 + d, src, wc_ref.at[other], ring[d])
    for i in (5, 6, 7, 8, 10, 11, 12, 13, 14, 15):
        copies[i].wait_recv()
    for i in range(16):
        copies[i].wait_send()
    keep_a.wait()
    keep_w.wait()
    keep_x.wait()


def gather_acts(acts_t, weight):
    width, rows = acts_t.shape
    vmem = pl.BlockSpec(memory_space=pltpu.VMEM)
    return pl.pallas_call(
        gather_kernel,
        out_shape=(
            jax.ShapeDtypeStruct((8, width, rows), bf16),
            jax.ShapeDtypeStruct((8, width, 128), bf16),
        ),
        in_specs=[vmem, vmem],
        out_specs=(vmem, vmem),
        scratch_shapes=[
            pltpu.VMEM((width, 512), bf16),
            pltpu.SemaphoreType.DMA((16,)),
            pltpu.SemaphoreType.DMA((16,)),
            pltpu.SemaphoreType.DMA((3,)),
        ],
        compiler_params=pltpu.CompilerParams(
            collective_id=0, has_side_effects=True, vmem_limit_bytes=32 * 1024 * 1024
        ),
    )(acts_t, weight)


def product_kernel(at_ref, wc_ref, part_ref, right_ref):
    t = lax.axis_index("tp")
    projected = mm(at_ref[...], wc_ref[...], TN).astype(bf16)
    for i in range(10):
        rows = pl.ds(i * 256, 256)
        own = at_ref[rows, :]
        wide = own.astype(f32)
        diag = jnp.sum(wide * wide, axis=1, keepdims=True)
        scaled = diag * wc_ref[rows, :].astype(f32)
        right_ref[rows, :] = SHRINK * mm(own, projected) + (1.0 - SHRINK) * scaled
    for s in range(NS):
        b = jnp.minimum(s * 8 + t, 54)
        k = 0
        for j in range(1, 10):
            k = k + (b >= 10 * j - j * (j - 1) // 2).astype(jnp.int32)
        i = b - (10 * k - k * (k - 1) // 2) + k
        left = at_ref[pl.ds(pl.multiple_of(i * 256, 256), 256), :]
        right = at_ref[pl.ds(pl.multiple_of(k * 256, 256), 256), :]
        part_ref[s] = mm(left, right, NT)


def products(at, wc):
    vmem = pl.BlockSpec(memory_space=pltpu.VMEM)
    return pl.pallas_call(
        product_kernel,
        out_shape=(
            jax.ShapeDtypeStruct((NS, 256, 256), f32),
            jax.ShapeDtypeStruct((2560, 128), f32),
        ),
        in_specs=[vmem, vmem],
        out_specs=(vmem, vmem),
        compiler_params=pltpu.CompilerParams(vmem_limit_bytes=40 * 1024 * 1024),
    )(at, wc)


def sum_spread_kernel(
    g_ref, r_ref, go_ref, ro_ref, g_pair, r_pair, g_in, r_in, g_own, r_own,
    send, recv, gsend, grecv, rsend, rrecv, own,
):
    x, y, z, c = place()
    coord = (x, y, z)
    q = (x % 2) * 4 + y
    pair = device(x, y, z, 1 - c)
    peers = []
    for d in range(1, 8):
        p = (q + d) % 8
        peers.append((p, device((x // 2) * 2 + p // 4, p % 4, z, c)))

    def along(axis, shift):
        moved = list(coord)
        moved[axis] = (moved[axis] + shift) % 4
        return device(*moved, c)

    ring = [[along(axis, shift) for shift in range(4)] for axis in range(3)]
    near = [ring[axis][shift] for axis in range(3) for shift in (1, 2, 3)]
    greet([pair] + [peer for _, peer in peers] + near)

    first = [
        remote(g_ref.at[:, 1 - c], g_pair, send.at[0], recv.at[0], pair),
        remote(r_ref.at[1 - c], r_pair, send.at[1], recv.at[1], pair),
    ]
    for copy in first:
        copy.start()
    second, third = [], []
    for d, (p, peer) in enumerate(peers):
        second.append(remote(g_pair.at[:, p], g_in.at[d], send.at[2 + d], recv.at[2 + d], peer))
        third.append(remote(r_pair.at[p], r_in.at[d], send.at[9 + d], recv.at[9 + d], peer))
    first[0].wait_recv()
    g_pair[...] = g_pair[...] + g_ref[:, c]
    for copy in second:
        copy.start()
    first[1].wait_recv()
    r_pair[...] = r_pair[...] + r_ref[c]
    for copy in third:
        copy.start()
    for copy in second:
        copy.wait_recv()
    g_sum = g_pair[:, q]
    for d in range(7):
        g_sum = g_sum + g_in[d]
    g_own[...] = g_sum
    started = first + second + third

    keep_g = pltpu.make_async_copy(g_own, go_ref.at[:, c, x, y, z], own.at[0])
    keep_r = pltpu.make_async_copy(r_own, ro_ref.at[c * 8 + q], own.at[1])
    keep_g.start()

    def turn(n, phase):
        return (PARTS[n][0] + phase) % 3

    def view(n, phase, value, half=None):
        axis, start, count, row = PARTS[n]
        index = list(coord)
        for earlier in range(phase):
            index[(axis + earlier) % 3] = pl.ds(0, 4)
        index[(axis + phase) % 3] = value
        index = [pl.ds(start, count), c] + index
        if row is not None:
            index.append(pl.ds(row, 8))
            if half is not None:
                index.append(pl.ds(128 * half, 128))
        elif half is not None:
            index.append(pl.ds(8 * half, 8))
        return go_ref.at[tuple(index)]

    def own_part(n):
        _, start, count, row = PARTS[n]
        if row is None:
            return g_own.at[pl.ds(start, count)]
        return g_own.at[pl.ds(start, count), pl.ds(row, 8)]

    def copy(ref, sems, i, peer, src=None):
        made = remote(ref if src is None else src, ref, sems[0].at[i], sems[1].at[i], peer)
        made.start()
        started.append(made)
        return made

    g_sems, r_sems = (gsend, grecv), (rsend, rrecv)
    order = (2, 1, 4, 0, 3)

    def spread_along(p, phase):
        axis = turn(p, phase)
        mine = view(p, phase, coord[axis])
        base = p * 14 + phase * 3
        source = own_part(p) if phase == 0 else None
        return [
            copy(mine, g_sems, base + n, ring[axis][shift], source)
            for n, shift in enumerate((2, 1, 3))
        ]

    flying = {p: spread_along(p, 0) for p in range(5)}
    keep_g.wait()
    for p in order:
        for made in flying[p]:
            made.wait_recv()
        flying[p] = spread_along(p, 1)
    for made in third:
        made.wait_recv()
    r_sum = r_pair[q]
    for d in range(7):
        r_sum = r_sum + r_in[d]
    r_own[...] = r_sum
    keep_r.start()
    r_copies = [
        copy(ro_ref.at[c * 8 + q], r_sems, d, peer, r_own) for d, (_, peer) in enumerate(peers)
    ]
    last = []
    for p in order:
        for made in flying[p]:
            made.wait_recv()
        axis = turn(p, 2)
        mine = view(p, 2, coord[axis])
        base = p * 14 + 6
        flying[p] = (
            copy(mine, g_sems, base, ring[axis][1]),
            copy(mine, g_sems, base + 1, ring[axis][3]),
        )
        last.append(copy(mine, g_sems, p * 14 + 10, pair))
    for p in order:
        axis = turn(p, 2)
        base = p * 14 + 6
        before, after = (coord[axis] + 3) % 4, (coord[axis] + 1) % 4
        one, two = flying[p]
        one.wait_recv()
        three = copy(view(p, 2, before, 0), g_sems, base + 2, ring[axis][1])
        two.wait_recv()
        four = copy(view(p, 2, after, 1), g_sems, base + 3, ring[axis][3])
        flying[p] = (three, four)
        last.append(copy(view(p, 2, before), g_sems, p * 14 + 11, pair))
        last.append(copy(view(p, 2, after), g_sems, p * 14 + 12, pair))
    keep_r.wait()
    for made in r_copies:
        made.wait_recv()
    last.append(copy(ro_ref.at[pl.ds(pl.multiple_of(c * 8, 8), 8)], r_sems, 7, pair))
    for p in order:
        axis = turn(p, 2)
        for made in flying[p]:
            made.wait_recv()
        far = (coord[axis] + 2) % 4
        last.append(copy(view(p, 2, far), g_sems, p * 14 + 13, pair))
    for made in last:
        made.wait_recv()
    for made in started:
        made.wait_send()


def sum_spread(part, right):
    hbm = pl.BlockSpec(memory_space=pl.ANY)
    vmem = pl.BlockSpec(memory_space=pltpu.VMEM)
    return pl.pallas_call(
        sum_spread_kernel,
        out_shape=(
            jax.ShapeDtypeStruct((NS, 2, 4, 4, 4, 16, 256), f32),
            jax.ShapeDtypeStruct((16, 160, 128), f32),
        ),
        in_specs=[vmem, vmem],
        out_specs=(hbm, hbm),
        scratch_shapes=[
            pltpu.VMEM((NS, 8, 16, 256), f32),
            pltpu.VMEM((8, 160, 128), f32),
            pltpu.VMEM((7, NS, 16, 256), f32),
            pltpu.VMEM((7, 160, 128), f32),
            pltpu.VMEM((NS, 16, 256), f32),
            pltpu.VMEM((160, 128), f32),
            pltpu.SemaphoreType.DMA((16,)),
            pltpu.SemaphoreType.DMA((16,)),
            pltpu.SemaphoreType.DMA((70,)),
            pltpu.SemaphoreType.DMA((70,)),
            pltpu.SemaphoreType.DMA((8,)),
            pltpu.SemaphoreType.DMA((8,)),
            pltpu.SemaphoreType.DMA((2,)),
        ],
        compiler_params=pltpu.CompilerParams(
            collective_id=3, has_side_effects=True, vmem_limit_bytes=40 * 1024 * 1024
        ),
    )(part.reshape(NS, 2, 8, 16, 256), right.reshape(2, 8, 160, 128))

N = 2560
NB = N // B
RC = 128
CLASSES = ((0, 3, 9), (3, 6, 6), (6, 10, 3))


def cut(k, width=B):
    return slice(k * B, k * B + width)


def prod(left, right, dims):
    lh, ll = left
    rh, rl = right
    return mm(lh, rh, dims) + (mm(ll, rh, dims) + mm(lh, rl, dims))


def chain(left, right, dims):
    lh, ll = left
    rh, rl = right
    axis = dims[0][1][0]
    return mm(jnp.concatenate([lh, ll, lh], 1), jnp.concatenate([rh, rh, rl], axis), dims)


def factor_kernel(
    g_hbm, r_ref, o_ref, g, low, y_low, y, w_low, diag, panel, y_panel,
    second, rest, l21_low, a1_low, low1_low, live, sems,
):
    row = lax.broadcasted_iota(jnp.int32, (B, B), 0)
    col = lax.broadcasted_iota(jnp.int32, (B, B), 1)

    copies = [pltpu.make_async_copy(g_hbm.at[s], g.at[s], sems.at[s]) for s in range(NS)]
    for copy in copies:
        copy.start()

    live[0] = 1

    def lanes(k):
        return pl.ds(pl.multiple_of(k * B, B), B)

    def gram(i, k):
        b = jnp.minimum(10 * k - k * (k - 1) // 2 + i - k, 54)
        s, t = b // 8, b % 8
        tile = g[s, :, pl.ds((t // 4) * 2, 2), :, t % 4].reshape(B, B)
        return tile

    def gram_diag(k):
        tile = gram(k, k)
        return jnp.where(row == col, tile, SHRINK * tile)

    def rows_of(i, width):
        return low[i, :B, :width], low[i, B:, :width]

    def put(i, k, value):
        h, l = split(value)
        low[i, :B, lanes(k)] = h
        low[i, B:, lanes(k)] = l

    def put_y(k, value):
        y[:, lanes(k)] = value
        if isinstance(k, int) and k == NB - 1:
            return
        h, l = split(value)
        y_low[:RC, lanes(k)] = h
        y_low[RC:, lanes(k)] = l

    def w_of(k):
        return w_low[k, :B, :], w_low[k, B:, :]

    def step(k, width, tiles):
        if width == CLASSES[0][1] * B - B:

            @pl.when(k == 1)
            def _():
                for copy in copies[2:]:
                    copy.wait()

        old, now = (k + 1) % 2, k % 2
        last = jnp.maximum(k - 1, 0)
        targets = [jnp.minimum(k + 1 + r, NB) for r in range(tiles)]
        early = tiles // 3 + 1
        here = rows_of(k, width)

        def update(i):
            panel[now, i] = SHRINK * gram(i, k) - prod(rows_of(i, width), here, NT)

        @pl.when(live[0] == 1)
        def _():
            w1 = split(inverse_factor(diag[:H, :H]))
            w_old = w_of(last)
            for i in targets:
                put(i, last, prod(split(panel[old, i]), w_old, NT))
            put_y(last, prod(split(y_panel[old]), w_old, NT))
            for i in targets[:early]:
                update(i)
            for part in range(2):
                first = part * B
                w_low[k, first : first + H, :H] = w1[part]
                w_low[k, first : first + H, H:] = jnp.zeros((H, H), bf16)

        def w1_of():
            return w_low[k, :H, :H], w_low[k, B : B + H, :H]

        @pl.when(live[0] == 1)
        def _():
            l21 = chain(split(diag[H:, :H]), w1_of(), NT)
            l21s = split(l21)
            l21_low[...] = l21
            second[...] = diag[H:, H:] - chain(l21s, l21s, NT)

        @pl.when(live[0] == 1)
        def _():
            w2 = split(inverse_factor(second[...]))
            for i in targets[early:]:
                update(i)
            y_rows = y_low[:RC, :width], y_low[RC:, :width]
            y_panel[now] = r_ref[lanes(k), :].T - prod(y_rows, here, NT)
            mine = rows_of(k + 1, width)
            after = gram_diag(k + 1) - prod(mine, mine, NT)
            value = panel[now, k + 1]
            a1 = chain(split(value[:, :H]), w1_of(), NT)
            a1s = split(a1)
            a1_low[...] = a1
            diag[...] = after - chain(a1s, a1s, NT)
            rest[...] = value[:, H:] - chain(a1s, split(l21_low[...]), NT)
            low1_low[...] = chain(split(l21_low[...]), w1_of(), NN)
            for part in range(2):
                first = part * B + H
                w_low[k, first : first + H, H:] = w2[part]

        @pl.when(live[0] == 1)
        def _():
            w2s = w_low[k, H:B, H:], w_low[k, B + H :, H:]
            a2s = split(chain(split(rest[...]), w2s, NT))
            diag[...] = diag[...] - chain(a2s, a2s, NT)
            own = lanes(jnp.minimum(k, NB - 2))
            a1s = split(a1_low[...])
            low[k + 1, :B, own] = jnp.concatenate([a1s[0], a2s[0]], 1)
            low[k + 1, B:, own] = jnp.concatenate([a1s[1], a2s[1]], 1)
            w21 = split(-chain(w2s, split(low1_low[...]), NN))
            for part in range(2):
                first = part * B + H
                w_low[k, first : first + H, :H] = w21[part]

    for lo, hi, _ in CLASSES:
        zeros = jnp.zeros((2 * B, (hi - 1 - lo) * B), bf16)
        for i in range(lo, NB + 1):
            low[i, :, lo * B : (hi - 1) * B] = zeros
        y_low[:, lo * B : (hi - 1) * B] = jnp.zeros((2 * RC, (hi - 1 - lo) * B), bf16)
    panel[1] = jnp.zeros((NB + 1, B, B), f32)
    y_panel[1] = jnp.zeros((RC, B), f32)
    w_low[0] = jnp.zeros((2 * B, B), bf16)
    panel[0, NB] = jnp.zeros((B, B), f32)

    for copy in copies[:2]:
        copy.wait()
    diag[...] = gram_diag(0)
    for lo, hi, tiles in CLASSES:

        def one(k, _):
            step(k, (hi - 1) * B, tiles)
            return 0

        lax.fori_loop(lo, hi, one, 0)
    put_y(NB - 1, prod(split(y_panel[(NB - 1) % 2]), w_of(NB - 1), NT))
    for k in range(NB - 1, -1, -1):
        x = prod(split(y[:, cut(k)]), w_of(k), NN)
        o_ref[cut(k), :] = x.T.astype(bf16)
        xs = split(x)
        for j in range(k - 1, -1, -1):
            tile = low[k, :B, cut(j)], low[k, B:, cut(j)]
            y[:, cut(j)] = y[:, cut(j)] - prod(xs, tile, NN)


def factor_solve(gram, right):
    return pl.pallas_call(
        factor_kernel,
        out_shape=jax.ShapeDtypeStruct((N, RC), bf16),
        in_specs=[pl.BlockSpec(memory_space=pl.ANY), pl.BlockSpec(memory_space=pltpu.VMEM)],
        out_specs=pl.BlockSpec(memory_space=pltpu.VMEM),
        scratch_shapes=[
            pltpu.VMEM((NS, 2, 4, 4, 4, 16, 256), f32),
            pltpu.VMEM((NB + 1, 2 * B, N - B), bf16),
            pltpu.VMEM((2 * RC, N - B), bf16),
            pltpu.VMEM((RC, N), f32),
            pltpu.VMEM((NB, 2 * B, B), bf16),
            pltpu.VMEM((B, B), f32),
            pltpu.VMEM((2, NB + 1, B, B), f32),
            pltpu.VMEM((2, RC, B), f32),
            pltpu.VMEM((H, H), f32),
            pltpu.VMEM((B, H), f32),
            pltpu.VMEM((H, H), f32),
            pltpu.VMEM((B, H), f32),
            pltpu.VMEM((H, H), f32),
            pltpu.SMEM((1,), jnp.int32),
            pltpu.SemaphoreType.DMA((NS,)),
        ],
        compiler_params=pltpu.CompilerParams(vmem_limit_bytes=60 * 1024 * 1024),
    )(gram, right)


def local(acts, weights):
    at, wc = gather_acts(acts[0].T, weights[0])
    part, right = products(at.reshape(N, -1), wc.reshape(N, RC))
    gram, right = sum_spread(part, right)
    return factor_solve(gram, right.reshape(N, RC))


def solution(mesh):
    in_specs = (P("member", None, "tp"), P("member", "tp", None))
    return jax.shard_map(
        local, mesh=mesh, in_specs=in_specs, out_specs=P(None, "tp"), check_vma=False
    )
```
